256 devices in a mesh: layer: 32 (over z, x_hi, core), feat: 8 (over x_lo, y).
Axes of the slice: x: 4 (x_hi: 2, x_lo: 2; x = x_hi * 2 + x_lo), y: 4, z: 8, core: 2. Of those that a mesh axis runs over, the one named last changes fastest.
Arguments:
- resid: bfloat16 [1024, 4096], P('layer', 'feat'), may hold values from -40 to 40
- target: bfloat16 [1024, 4096], P('layer', 'feat'), may hold values from -6 to 6
- feat_idx: int32 [1024, 64], P('layer'), may hold values from 0 to 32767, as said below
- enc_weight: bfloat16 [65536, 4096], P(('layer', 'feat')), may hold values from -0.09375 to 0.09375
- enc_bias: float32 [65536], P(('layer', 'feat')), may hold values from -3 to 3
- dec_weight: bfloat16 [65536, 8192], P(('layer', 'feat')), may hold values from -0.5 to 0.5
- enc_second: float32 [65536], P(('layer', 'feat')), may hold values from 0.1 to 10
- dec_second: float32 [65536], P(('layer', 'feat')), may hold values from 0.1 to 10
Outputs:
- enc_step: bfloat16 [65536, 4096], P(('layer', 'feat'))
- dec_step: bfloat16 [65536, 8192], P(('layer', 'feat'))
- enc_second_new: float32 [65536], P(('layer', 'feat'))
- dec_second_new: float32 [65536], P(('layer', 'feat'))
The draws below stay inside these ranges and needn't reach their ends.
Inputs may be any that keep to these rules, and one draw needn't show every extreme that they name: `feat_idx`: each row names 64 different features.
All inputs are finite; a program needn't handle non-finite values.
Results may differ from the reference program's by a relative error of at most 0.02.
Values may be sent and summed in bfloat16 or wider, within the bound.
No kernel may reach another device: no remote copies, remote signals or barrier semaphores. Data moves between devices by JAX's collectives and lax.ppermute only.
A program may use at most 128 MiB of HBM per device.

```python
import math
import jax
import jax.numpy as jnp
from jax import lax

D = 4096
K = 64
WINDOW = 2
TOKENS = 512
LAYERS = 2
FEATS = 32768


def draw_resid(key, part):
    key = jax.random.fold_in(key, 11)
    base_key, row_key, col_key = jax.random.split(key, 3)
    total_rows = LAYERS * TOKENS
    base = jax.random.normal(base_key, (total_rows, D), jnp.float32)
    spread = 1.15
    row_scale = jnp.exp(jax.random.uniform(row_key, (total_rows, 1), jnp.float32, -spread, spread))
    col_scale = jnp.exp(jax.random.uniform(col_key, (1, D), jnp.float32, -spread, spread))
    return jnp.clip(base * row_scale * col_scale, -40.0, 40.0).astype(jnp.bfloat16)


def draw_feat_idx(key, part):
    key = jax.random.fold_in(key, 23)
    start_key, pick_key = jax.random.split(key, 2)
    total_rows = LAYERS * TOKENS
    bucket = FEATS // K
    starts = jax.random.randint(start_key, (total_rows, 1), 0, FEATS, jnp.int32)
    uniform_pick = jax.random.randint(pick_key, (total_rows, K), 0, bucket, jnp.int32)
    picks = uniform_pick * uniform_pick // bucket
    starts = starts.at[0, 0].set(0)
    picks = picks.at[0, 0].set(0)
    picks = picks.at[0, K - 1].set(bucket - 1)
    slots = jnp.arange(K, dtype=jnp.int32)[None, :] * bucket
    return ((starts + slots + picks) % FEATS).astype(jnp.int32)


def shard_levels(rng, extent, cuts, low, high):
    factor_of = 1.0
    for dim, blocks in cuts:
        steps = jax.random.uniform(jax.random.fold_in(jax.random.fold_in(rng, 6), dim), (blocks,), jnp.float32, low / len(cuts), high / len(cuts))
        factor_of = factor_of * jnp.repeat(jnp.exp(steps), extent[dim] // blocks).reshape((-1,) + (1,) * (len(extent) - 1 - dim))
    return factor_of


def gaussian(key, dims, width, bound, cuts=(), kind=jnp.bfloat16):
    level = shard_levels(key, dims, cuts, -0.22, 0.18) if cuts else 1.0
    values = jax.random.normal(key, dims, jnp.float32) * width * level
    return jnp.minimum(jnp.maximum(values, -bound), bound).astype(kind)


def setup_inputs(seed: int = 0) -> dict:
    key_of = jax.random.split(jax.random.key(seed), 9)
    resid = draw_resid(jax.random.fold_in(key_of[8], 71), 0)
    target = gaussian(key_of[1], (LAYERS * TOKENS, D), 1.0, 6.0, ((0, 32), (1, 8)))
    feat_idx = draw_feat_idx(jax.random.fold_in(key_of[8], 71), 0)
    enc_weight = gaussian(key_of[3], (LAYERS * FEATS, D), D ** -0.5, 0.09375, ((0, 256),))
    enc_bias = gaussian(key_of[4], (LAYERS * FEATS,), 0.5, 3.0, ((0, 256),), jnp.float32)
    dec_weight = gaussian(key_of[5], (LAYERS * FEATS, WINDOW * D), (WINDOW * K) ** -0.5, 0.5, ((0, 256),))
    enc_second = jnp.clip(jnp.exp(math.log(10.0) - 4.6051702 * jax.random.uniform(key_of[6], (LAYERS * FEATS,), jnp.float32) ** shard_levels(key_of[6], (LAYERS * FEATS,), ((0, 256),), -0.2, 0.2)), 0.1, 10.0)
    dec_second = jnp.clip(jnp.exp(math.log(10.0) - 4.6051702 * jax.random.uniform(key_of[7], (LAYERS * FEATS,), jnp.float32) ** shard_levels(key_of[7], (LAYERS * FEATS,), ((0, 256),), -0.2, 0.2)), 0.1, 10.0)
    return dict(resid=resid, target=target, feat_idx=feat_idx, enc_weight=enc_weight, enc_bias=enc_bias, dec_weight=dec_weight, enc_second=enc_second, dec_second=dec_second)


EPSILON = 1e-08
DECAY_RATE = 0.99

def in_blocks(array):
    return array.reshape((array.shape[0] // 8, 8) + array.shape[1:])

def accumulate(chosen, weights, values, row_width):

    def add_block(total, triple):
        rows_block, weight_block, value_block = triple
        outer = weight_block.astype(jnp.float32)[:, :, None] * value_block.astype(jnp.float32)[:, None, :]
        return (total.at[rows_block.reshape(-1)].add(outer.reshape(-1, row_width)), None)
    total = jnp.zeros((FEATS, row_width), jnp.float32)
    total, unused = lax.scan(add_block, total, (in_blocks(chosen), in_blocks(weights), in_blocks(values)))
    return total

def adam_rows(grad, second, touched):
    mean_square = lax.optimization_barrier(jnp.mean(grad * grad, axis=1))
    renewed = jnp.where(touched, DECAY_RATE * second + (1.0 - DECAY_RATE) * mean_square, second)
    step = jnp.where(touched[:, None], -grad / (jnp.sqrt(renewed)[:, None] + EPSILON), jnp.zeros_like(grad))
    return (step.astype(jnp.bfloat16), renewed)

def reference(resid, target, feat_idx, enc_weight, enc_bias, dec_weight, enc_second, dec_second):
    row_width = WINDOW * D
    activity = []
    totals = [jnp.zeros((TOKENS, D), jnp.float32) for target_pos in range(LAYERS)]
    for layer_pos in range(LAYERS):
        first_row = layer_pos * TOKENS
        resid_block = resid[first_row:first_row + TOKENS]
        chosen = (feat_idx[first_row:first_row + TOKENS] + layer_pos * FEATS).astype(jnp.int32)

        def encode(pair):
            resid_rows, chosen_rows = pair
            encoder = enc_weight[chosen_rows].astype(jnp.float32)
            preact = jnp.einsum('td,tkd->tk', resid_rows.astype(jnp.float32), encoder)
            values = (preact + enc_bias[chosen_rows]).astype(jnp.bfloat16)
            decoder = dec_weight[chosen_rows].astype(jnp.float32)
            decoded = jnp.einsum('tk,tkc->tc', values.astype(jnp.float32), decoder)
            return (values, decoded)
        values, decoded = lax.map(encode, (in_blocks(resid_block), in_blocks(chosen)))
        values = values.reshape(TOKENS, K)
        decoded = decoded.reshape(TOKENS, row_width)
        activity.append(values)
        for slot_pos in range(WINDOW):
            if layer_pos + slot_pos < LAYERS:
                totals[layer_pos + slot_pos] = totals[layer_pos + slot_pos] + decoded[:, slot_pos * D:(slot_pos + 1) * D]
    errors = []
    for target_pos in range(LAYERS):
        first_row = target_pos * TOKENS
        errors.append((totals[target_pos] - target[first_row:first_row + TOKENS].astype(jnp.float32)).astype(jnp.bfloat16))
    enc_steps, dec_steps, enc_news, dec_news = ([], [], [], [])
    for layer_pos in range(LAYERS):
        first_row = layer_pos * TOKENS
        resid_block = resid[first_row:first_row + TOKENS]
        local_chosen = feat_idx[first_row:first_row + TOKENS].astype(jnp.int32)
        chosen = (local_chosen + layer_pos * FEATS).astype(jnp.int32)
        pieces = []
        for slot_pos in range(WINDOW):
            if layer_pos + slot_pos < LAYERS:
                pieces.append(errors[layer_pos + slot_pos])
            else:
                pieces.append(jnp.zeros((TOKENS, D), jnp.bfloat16))
        err_cat = jnp.concatenate(pieces, axis=1)

        def backward(pair):
            err_rows, chosen_rows = pair
            decoder = dec_weight[chosen_rows].astype(jnp.float32)
            return jnp.einsum('tc,tkc->tk', err_rows.astype(jnp.float32), decoder).astype(jnp.bfloat16)
        feature_grad = lax.map(backward, (in_blocks(err_cat), in_blocks(chosen))).reshape(TOKENS, K)
        grad_dec = accumulate(local_chosen, activity[layer_pos], err_cat, row_width)
        grad_enc = accumulate(local_chosen, feature_grad, resid_block, D)
        counts = jnp.zeros((FEATS,), jnp.int32).at[local_chosen.reshape(-1)].add(1)
        touched = counts > 0
        rows_here = slice(layer_pos * FEATS, (layer_pos + 1) * FEATS)
        enc_piece, enc_new = adam_rows(grad_enc, enc_second[rows_here], touched)
        dec_piece, dec_new = adam_rows(grad_dec, dec_second[rows_here], touched)
        enc_steps.append(enc_piece)
        dec_steps.append(dec_piece)
        enc_news.append(enc_new)
        dec_news.append(dec_new)
    return (jnp.concatenate(enc_steps, 0), jnp.concatenate(dec_steps, 0), jnp.concatenate(enc_news, 0), jnp.concatenate(dec_news, 0))
```

```python
import functools
import jax
import jax.numpy as jnp
from jax import lax
from jax.experimental import pallas as pl
from jax.experimental.pallas import tpu as pltpu
from jax.sharding import Mesh, PartitionSpec as P

EPSILON = 1e-08
DECAY_RATE = 0.99
X = ("xh", "xl")
F32 = jnp.float32
BF16 = jnp.bfloat16
ANY = pl.BlockSpec(memory_space=pl.ANY)
VMEM = pl.BlockSpec(memory_space=pltpu.VMEM)
PARAMS = pltpu.CompilerParams(vmem_limit_bytes=56 * 2**20)


def position():
    x = lax.axis_index("xh") * 2 + lax.axis_index("xl")
    return lax.axis_index("c"), x, lax.axis_index("y")


def from_ahead(value, axis, steps, size=4):
    return lax.ppermute(value, axis, [((i + steps) % size, i) for i in range(size)])


def to_ahead(value, axis, steps, size=4):
    return from_ahead(value, axis, -steps, size)


def swap_cores(value):
    return lax.ppermute(value, "c", [(0, 1), (1, 0)])


def in_order(parts, own):
    stack = jnp.stack(parts + parts[:-1])
    return lax.dynamic_slice_in_dim(stack, (4 - own) % 4, 4, 0)


def direct_gather(value, axis):
    far = from_ahead(value, axis, 2)
    return [value, from_ahead(value, axis, 1), far, from_ahead(value, axis, 3)]


def relay_gather(value, axis):
    half = value.shape[0] // 2
    plus = from_ahead(value, axis, 1)
    minus = from_ahead(value, axis, 3)
    far_a = from_ahead(plus[:half], axis, 1)
    far_b = from_ahead(minus[half:], axis, 3)
    return [value, plus, far_a, far_b, minus]


def call(kernel, outs, scratch, in_specs, out_specs, flops, moved, name):
    return pl.pallas_call(
        kernel,
        out_shape=outs,
        in_specs=in_specs,
        out_specs=out_specs,
        scratch_shapes=scratch,
        compiler_params=PARAMS,
        cost_estimate=pl.CostEstimate(flops=flops, bytes_accessed=moved, transcendentals=0),
        name=name,
    )


def dot_nt(a, b):
    return lax.dot_general(a, b, (((1,), (1,)), ((), ())), preferred_element_type=F32)


def dot_nn(a, b):
    return jnp.dot(a, b, preferred_element_type=F32)


def shape(dims, kind=BF16):
    return jax.ShapeDtypeStruct(dims, kind)


def mask_kernel(base_ref, idx_ref, out_ref):
    chosen, tokens = idx_ref.shape
    n_feat = out_ref.shape[1]
    step = 32
    for part in range(2):
        base = base_ref[part]

        def chunk(i, carry):
            first = pl.multiple_of(i * step, step)
            names = lax.broadcasted_iota(jnp.int32, (step, tokens), 0) + (base + first)
            found = jnp.zeros((step, tokens), F32)
            for k in range(chosen):
                found = jnp.where(idx_ref[pl.ds(k, 1), :] == names, 1.0, found)
            out_ref[part, pl.ds(first, step), :] = found.astype(BF16)
            return carry

        lax.fori_loop(0, n_feat // step, chunk, 0)


def place_copies(refs, dest, sems, row_base, width, shift, by_x, x, y):
    own, plus, far_a, far_b, minus = refs
    half = far_a.shape[0]
    rows = own.shape[1]
    parts = []
    for i in range(2 * half):
        parts.append((own, i, 0, i))
        parts.append((plus, i, 1, i))
        parts.append((minus, i, 3, i))
        if i < half:
            parts.append((far_a, i, 2, i))
        else:
            parts.append((far_b, i - half, 2, i))
    copies = []
    tile = 2 * width if shift is not None else width
    for n, (ref, slot, ring, inner) in enumerate(parts):
        if by_x:
            px, py = (x + ring) % 4, (y + inner) % 4
        else:
            px, py = (x + inner) % 4, (y + ring) % 4
        row = pl.multiple_of(row_base + (px // 2) * rows, 128)
        col = pl.multiple_of((px % 2) * (4 * tile) + py * tile + (shift or 0), 256)
        copies.append(
            pltpu.make_async_copy(
                ref.at[slot], dest.at[pl.ds(row, rows), pl.ds(col, width)], sems.at[n]
            )
        )
    return copies


def encode_kernel(*refs):
    a_refs, b_refs = refs[0:5], refs[5:10]
    enc_own, enc_other, bias_ref, mask_ref, act_ref, x_out, xs, sems, out_sem = refs[10:]
    c, x, y = position()
    copies = place_copies(a_refs, xs, sems.at[0], 0, 256, 0, True, x, y)
    copies += place_copies(b_refs, xs, sems.at[1], 0, 256, 256, False, x, y)
    for copy in copies:
        copy.start()
    for copy in copies:
        copy.wait()
    back = pltpu.make_async_copy(xs, x_out, out_sem)
    back.start()
    tokens = xs.shape[0]
    first = pl.multiple_of(c * tokens, 256)
    for part, weight in enumerate((enc_own, enc_other)):
        pre = dot_nt(weight[...], xs[...]) + bias_ref[part]
        chosen = mask_ref[part, :, pl.ds(first, tokens)].astype(F32)
        act_ref[part] = jnp.where(chosen > 0, pre, 0.0).astype(BF16)
    back.wait()


def decode_kernel(half_ref, recv_ref, dec_hbm, dec_other, *rest):
    outs = rest[:10]
    at, dec_own, a_blk, b_blk, sem, out_sems = rest[10:]
    c, x, y = position()
    width = dec_own.shape[1]
    load = pltpu.make_async_copy(
        dec_hbm.at[:, pl.ds(pl.multiple_of(c * width, 256), width)], dec_own, sem
    )
    load.start()
    mine = pl.multiple_of(c * 256, 256)
    other = pl.multiple_of((1 - c) * 256, 256)
    at[pl.ds(mine, 256), 0:256] = half_ref[0].astype(F32).T.astype(BF16)
    at[pl.ds(mine, 256), 256:512] = half_ref[1].astype(F32).T.astype(BF16)
    at[pl.ds(other, 256), 0:256] = recv_ref[1].astype(F32).T.astype(BF16)
    at[pl.ds(other, 256), 256:512] = recv_ref[0].astype(F32).T.astype(BF16)
    load.wait()

    def chunk(j, carry):
        cols = pl.ds(pl.multiple_of(j * 512, 512), 512)
        part = dot_nn(at[:, 0:256], dec_own[:, cols]) + dot_nn(at[:, 256:512], dec_other[:, cols])
        part = part.astype(BF16)
        xl, py = j // 4, j % 4
        a_cols = pl.ds(pl.multiple_of(py * 512, 512), 512)
        for xh in range(2):
            rel = (xh * 2 + xl - x + 4) % 4
            a_blk[rel, :, a_cols] = part[xh * 128 : (xh + 1) * 128]
        rel_y = (py - y + 4) % 4
        b_blk[rel_y, :, pl.ds(pl.multiple_of(xl * 512, 512), 512)] = part[256:512]
        return carry

    lax.fori_loop(0, 8, chunk, 0)
    copies = []
    for blk, (own, r1p, r1m, r2p, r2m) in ((a_blk, outs[:5]), (b_blk, outs[5:])):
        h = blk.shape[1] // 2
        lo, hi = pl.ds(0, h), pl.ds(h, h)
        copies += [
            (blk.at[2, lo], r1p.at[0]),
            (blk.at[1, hi], r1p.at[1]),
            (blk.at[2, hi], r1m.at[0]),
            (blk.at[3, lo], r1m.at[1]),
            (blk.at[1, lo], r2p),
            (blk.at[3, hi], r2m),
            (blk.at[0], own),
        ]
    started = [
        pltpu.make_async_copy(src, dst, out_sems.at[n]) for n, (src, dst) in enumerate(copies)
    ]
    for copy in started:
        copy.start()
    for copy in started:
        copy.wait()


def relay_scatter(outs, axis):
    own, r1p, r1m, r2p, r2m = outs
    got_p = to_ahead(r1p, axis, 1)
    got_m = to_ahead(r1m, axis, 3)
    next_p = (r2p.astype(F32) + got_p[0].astype(F32)).astype(BF16)
    next_m = (r2m.astype(F32) + got_m[0].astype(F32)).astype(BF16)
    return [own, got_p, got_m, to_ahead(next_p, axis, 1), to_ahead(next_m, axis, 3)]


def second_kernel(*refs):
    a, b = refs[:5], refs[5:10]
    a_out, b_out = refs[10:14], refs[14:18]
    a_sum, b_sum, sems = refs[18:]
    c, x, y = position()
    for (own, got_p, got_m, last_p, last_m), total in ((a, a_sum), (b, b_sum)):
        h = own.shape[0] // 2
        total[0:h] = (
            own[0:h].astype(F32) + last_p[...].astype(F32) + got_m[1].astype(F32)
        ).astype(BF16)
        total[h:] = (
            own[h:].astype(F32) + got_p[1].astype(F32) + last_m[...].astype(F32)
        ).astype(BF16)
    copies = []
    for d in range(4):
        py, px = (y + d) % 4, (x + d) % 4
        copies.append((a_sum.at[:, pl.ds(pl.multiple_of(py * 512, 512), 512)], a_out[d]))
        rows = pl.ds(pl.multiple_of((px // 2) * 128, 128), 128)
        cols = pl.ds(pl.multiple_of((px % 2) * 512, 512), 512)
        copies.append((b_sum.at[rows, cols], b_out[d]))
    started = [
        pltpu.make_async_copy(src, dst, sems.at[n]) for n, (src, dst) in enumerate(copies)
    ]
    for copy in started:
        copy.start()
    for copy in started:
        copy.wait()


def backward_kernel(*refs):
    a_refs, b_refs = refs[0:5], refs[5:10]
    half_ref, recv_ref, dec_hbm, dec_other = refs[10:14]
    d_own, d_other, g_own, g_other, sq_own, sq_other = refs[14:20]
    err, dec_own, af, sems, sem = refs[20:]
    c, x, y = position()
    copies = place_copies(a_refs, err, sems.at[0], 0, 512, None, True, x, y)
    copies += place_copies(b_refs, err, sems.at[1], 256, 512, None, False, x, y)
    for copy in copies:
        copy.start()
    width = dec_own.shape[1]
    load = pltpu.make_async_copy(
        dec_hbm.at[:, pl.ds(pl.multiple_of(c * width, 256), width)], dec_own, sem
    )
    load.start()
    mine = pl.ds(pl.multiple_of(c * 256, 256), 256)
    other = pl.ds(pl.multiple_of((1 - c) * 256, 256), 256)
    af[0, :, mine] = half_ref[0]
    af[1, :, mine] = half_ref[1]
    af[0, :, other] = recv_ref[1]
    af[1, :, other] = recv_ref[0]
    for ref in (d_own, d_other, sq_own, sq_other):
        ref[...] = jnp.zeros_like(ref)
    for copy in copies:
        copy.wait()
    load.wait()

    def chunk(j, carry):
        cols = pl.ds(pl.multiple_of(j * 512, 512), 512)
        block = err[:, cols]
        d_own[...] += dot_nt(dec_own[:, cols], block)
        d_other[...] += dot_nt(dec_other[:, cols], block)
        g = dot_nn(af[0], block)
        g_own[:, cols] = g.astype(BF16)
        sq_own[...] += jnp.sum(g * g, axis=1, keepdims=True)
        g = dot_nn(af[1], block)
        g_other[:, cols] = g.astype(BF16)
        sq_other[...] += jnp.sum(g * g, axis=1, keepdims=True)
        return carry

    lax.fori_loop(0, 8, chunk, 0)


def step_kernel(
    d_mine, d_got, mask_ref, x_own, x_other, g_own, g_got, sq_mine, sq_got, esec, dsec,
    enc_step, dec_step, enc_new, dec_new, genc, dact, scaled, sems,
):
    c, x, y = position()
    chosen = mask_ref[0].astype(F32)
    touched = jnp.max(chosen, axis=1, keepdims=True) > 0
    width = genc.shape[1]
    v_dec = jnp.where(
        touched,
        DECAY_RATE * dsec[...] + (1.0 - DECAY_RATE) * ((sq_mine[...] + sq_got[...]) / (2 * width)),
        dsec[...],
    )
    dec_new[...] = v_dec
    rate = jnp.where(touched, -1.0 / (jnp.sqrt(v_dec) + EPSILON), 0.0)
    scaled[0] = (g_own[...].astype(F32) * rate).astype(BF16)
    scaled[1] = (g_got[...].astype(F32) * rate).astype(BF16)
    copies = []
    for n, slot in enumerate((c, 1 - c)):
        cols = pl.ds(pl.multiple_of(slot * width, 256), width)
        copy = pltpu.make_async_copy(scaled.at[n], dec_step.at[:, cols], sems.at[n])
        copy.start()
        copies.append(copy)
    dact[...] = jnp.where(chosen > 0, d_mine[...] + d_got[...], 0.0).astype(BF16)
    mine = pl.ds(pl.multiple_of(c * 256, 256), 256)
    other = pl.ds(pl.multiple_of((1 - c) * 256, 256), 256)

    def chunk(j, total):
        cols = pl.ds(pl.multiple_of(j * 512, 512), 512)
        g = dot_nn(dact[:, mine], x_own[:, cols]) + dot_nn(dact[:, other], x_other[:, cols])
        genc[:, cols] = g
        return total + jnp.sum(g * g, axis=1, keepdims=True)

    square = lax.fori_loop(0, width // 512, chunk, jnp.zeros((genc.shape[0], 1), F32))
    v_enc = jnp.where(
        touched, DECAY_RATE * esec[...] + (1.0 - DECAY_RATE) * (square / width), esec[...]
    )
    enc_new[...] = v_enc
    rate = jnp.where(touched, -1.0 / (jnp.sqrt(v_enc) + EPSILON), 0.0)
    enc_step[...] = (genc[...] * rate).astype(BF16)
    for copy in copies:
        copy.wait()


def body(resid, target, feat_idx, enc_weight, enc_bias, dec_weight, enc_second, dec_second):
    l, z = lax.axis_index("l"), lax.axis_index("z")
    xh, xl, c, y = (lax.axis_index(n) for n in ("xh", "xl", "c", "y"))
    is_one = c == 1
    n_f, width = enc_weight.shape

    idx = feat_idx
    idx_z = in_order(direct_gather(idx, "z"), z)
    other = lax.ppermute(idx_z, "xh", [(0, 1), (1, 0)])
    idx_x = jnp.where(xh == 1, jnp.stack([other, idx_z]), jnp.stack([idx_z, other]))
    other = swap_cores(idx_x)
    idx_c = jnp.where(is_one, jnp.stack([other, idx_x]), jnp.stack([idx_x, other]))
    idx_t = idx_c.reshape(512, 64).T
    feat = xl * 4 + y
    member = z * 4 + xh * 2 + c
    mate = z * 4 + xh * 2 + (1 - c)
    bases = jnp.stack([(member * 8 + feat) * n_f, (mate * 8 + feat) * n_f]).astype(jnp.int32)
    mask = call(
        mask_kernel,
        shape((2, n_f, 512)),
        [],
        [pl.BlockSpec(memory_space=pltpu.SMEM), VMEM],
        VMEM,
        2 * 64 * n_f * 512 * 20,
        2**20,
        "mask",
    )(bases, idx_t)

    enc_other = swap_cores(enc_weight)
    bias_other = swap_cores(enc_bias)
    dec_send = lax.dynamic_slice_in_dim(dec_weight, (1 - c) * width, width, 1)
    dec_other = swap_cores(dec_send)
    bias = jnp.stack([enc_bias, bias_other])[:, :, None]

    x_z = in_order(direct_gather(resid, "z"), z).reshape(128, 512)
    a1 = jnp.stack(direct_gather(x_z[:, :256], "y"))
    b1 = jnp.stack(direct_gather(x_z[:, 256:], X))
    a2 = relay_gather(a1, X)
    b2 = relay_gather(b1, "y")
    act_half, x_own = call(
        encode_kernel,
        (shape((2, n_f, 256)), shape((256, width))),
        [
            pltpu.VMEM((256, width), BF16),
            pltpu.SemaphoreType.DMA((2, 16)),
            pltpu.SemaphoreType.DMA,
        ],
        [ANY] * 10 + [VMEM] * 4,
        (VMEM, ANY),
        2 * 512 * 256 * width,
        8 * 2**20,
        "encode",
    )(*a2, *b2, enc_weight, enc_other, bias, mask)
    act_recv = swap_cores(act_half)
    x_other = swap_cores(x_own)

    blocks = []
    for rows, cols in ((128, 2048), (256, 1024)):
        h = rows // 2
        blocks += [
            shape((rows, cols)), shape((2, h, cols)), shape((2, h, cols)),
            shape((h, cols)), shape((h, cols)),
        ]
    outs = call(
        decode_kernel,
        tuple(blocks),
        [
            pltpu.VMEM((512, 512), BF16),
            pltpu.VMEM((n_f, width), BF16),
            pltpu.VMEM((4, 128, 2048), BF16),
            pltpu.VMEM((4, 256, 1024), BF16),
            pltpu.SemaphoreType.DMA,
            pltpu.SemaphoreType.DMA((14,)),
        ],
        [VMEM, VMEM, ANY, VMEM],
        (ANY,) * 10,
        2 * 512 * 512 * width,
        10 * 2**20,
        "decode",
    )(act_half, act_recv, dec_weight, dec_other)
    a3 = relay_scatter(outs[:5], X)
    b3 = relay_scatter(outs[5:], "y")
    parts = call(
        second_kernel,
        (shape((128, 512)),) * 8,
        [
            pltpu.VMEM((128, 2048), BF16),
            pltpu.VMEM((256, 1024), BF16),
            pltpu.SemaphoreType.DMA((8,)),
        ],
        [VMEM] * 10,
        (ANY,) * 8,
        2**21,
        4 * 2**20,
        "second",
    )(*a3, *b3)

    def direct_scatter(blocks, axis):
        far = to_ahead(blocks[2], axis, 2)
        got = [blocks[0], to_ahead(blocks[1], axis, 1), far, to_ahead(blocks[3], axis, 3)]
        return sum(g.astype(F32) for g in got)

    a4 = direct_scatter(parts[:4], "y").reshape(4, 32, 512)
    b4 = direct_scatter(parts[4:], X).reshape(4, 32, 512)
    both = jnp.stack([a4, b4], 1)
    twice = jnp.concatenate([both, both[:3]])
    own_z = lax.dynamic_slice_in_dim(twice, z, 4, 0)
    z_parts = [own_z[0]] + [own_z[d].astype(BF16) for d in range(1, 4)]
    total = direct_scatter(z_parts, "z")

    other = swap_cores(target)
    tgt = jnp.where(is_one, jnp.stack([other, target]), jnp.stack([target, other]))
    tgt_next = lax.ppermute(tgt, ("l", "c"), [(2, 1)])
    tgt = jnp.where(is_one, tgt_next, tgt)
    peer = lax.ppermute(total.astype(BF16), ("l", "c"), [(1, 2), (2, 1)])
    err = (total + peer.astype(F32) - tgt.astype(F32)).astype(BF16)
    err = jnp.where((l == 1) & is_one, jnp.zeros_like(err), err)

    err_z = in_order(direct_gather(err, "z"), z)
    a5 = jnp.stack(direct_gather(err_z[:, 0].reshape(128, 512), "y"))
    b5 = jnp.stack(direct_gather(err_z[:, 1].reshape(128, 512), X))
    a6 = relay_gather(a5, X)
    b6 = relay_gather(b5, "y")
    d_own, d_other, g_own, g_other, sq_own, sq_other = call(
        backward_kernel,
        (
            shape((n_f, 512), F32), shape((n_f, 512), F32),
            shape((n_f, width)), shape((n_f, width)),
            shape((n_f, 1), F32), shape((n_f, 1), F32),
        ),
        [
            pltpu.VMEM((512, width), BF16),
            pltpu.VMEM((n_f, width), BF16),
            pltpu.VMEM((2, n_f, 512), BF16),
            pltpu.SemaphoreType.DMA((2, 16)),
            pltpu.SemaphoreType.DMA,
        ],
        [ANY] * 10 + [VMEM, VMEM, ANY, VMEM],
        (VMEM,) * 6,
        4 * 512 * 512 * width,
        14 * 2**20,
        "backward",
    )(*a6, *b6, act_half, act_recv, dec_weight, dec_other)
    d_got = swap_cores(d_other)
    g_got = swap_cores(g_other)
    sq_got = swap_cores(sq_other)
    enc_step, dec_step, enc_new, dec_new = call(
        step_kernel,
        (
            shape((n_f, width)), shape((n_f, 2 * width)),
            shape((n_f, 1), F32), shape((n_f, 1), F32),
        ),
        [
            pltpu.VMEM((n_f, width), F32),
            pltpu.VMEM((n_f, 512), BF16),
            pltpu.VMEM((2, n_f, width), BF16),
            pltpu.SemaphoreType.DMA((2,)),
        ],
        [VMEM] * 11,
        (VMEM, ANY, VMEM, VMEM),
        2 * 512 * 256 * width,
        14 * 2**20,
        "steps",
    )(
        d_own, d_got, mask, x_own, x_other, g_own, g_got, sq_own, sq_got,
        enc_second[:, None], dec_second[:, None],
    )
    return enc_step, dec_step, enc_new[:, 0], dec_new[:, 0]


def solution(mesh):
    devices = mesh.devices.reshape(2, 4, 2, 2, 2, 4)
    fine = Mesh(devices, ("l", "z", "xh", "c", "xl", "y"))
    rows, cols = ("l", "z", "xh", "c"), ("xl", "y")
    in_specs = (
        P(rows, cols),
        P(rows, cols),
        P(rows, None),
        P(rows + cols, None),
        P(rows + cols),
        P(rows + cols, None),
        P(rows + cols),
        P(rows + cols),
    )
    out_specs = (P(rows + cols, None), P(rows + cols, None), P(rows + cols), P(rows + cols))
    return jax.shard_map(body, mesh=fine, in_specs=in_specs, out_specs=out_specs, check_vma=False)
```

```python
import jax
import jax.numpy as jnp
from jax import lax
from jax.experimental import pallas as pl
from jax.experimental.pallas import tpu as pltpu
from jax.sharding import Mesh, PartitionSpec as P

EPSILON = 1e-08
DECAY_RATE = 0.99
F32 = jnp.float32
BF16 = jnp.bfloat16
ANY = pl.BlockSpec(memory_space=pl.ANY)
VMEM = pl.BlockSpec(memory_space=pltpu.VMEM)
SMEM = pl.BlockSpec(memory_space=pltpu.SMEM)
DMA = pltpu.SemaphoreType.DMA
PLANE = ("xh", "c", "xl", "y")


def ring_ahead(which, steps):
    ahead = []
    for place in range(32):
        xh, c, xl, y = place // 16, place // 8 % 2, place // 4 % 2, place % 4
        x = xh * 2 + xl
        if (which == 1) == (c == 0):
            x = (x + steps) % 4
        else:
            y = (y + steps) % 4
        ahead.append(((x // 2) * 2 + c) * 8 + (x % 2) * 4 + y)
    return ahead


def ring_get(value, which, steps):
    ahead = ring_ahead(which, steps)
    return lax.ppermute(value, PLANE, [(ahead[i], i) for i in range(32)])


def ring_put(value, which, steps):
    return ring_get(value, which, -steps)


def z_get(value, steps):
    return lax.ppermute(value, "z", [((i + steps) % 4, i) for i in range(4)])


def swap_cores(value):
    return lax.ppermute(value, "c", [(0, 1), (1, 0)])


def gather(value, get):
    far = get(value, 2)
    return [value, get(value, 1), far, get(value, 3)]


def place():
    x = lax.axis_index("xh") * 2 + lax.axis_index("xl")
    return lax.axis_index("c"), x, lax.axis_index("y")


def tile_at(c, x, y, d1, d2):
    tx = (x + jnp.where(c == 0, d1, d2)) % 4
    ty = (y + jnp.where(c == 0, d2, d1)) % 4
    return tx // 2, (tx % 2) * 4 + ty


def tile_in_pair(c, x, d1s, i, d2):
    tx = (x + jnp.where(c == 0, d1s[i], d2)) % 4
    return tx // 2, jnp.where(c == 0, d2, i * 2 + tx % 2)


def pair_block(c, x, y, d1s, jj):
    by_x = ((x + d1s[0]) % 2) * 4 + (y + jj) % 4
    by_y = (jj % 2) * 4 + (y + d1s[jj // 2]) % 4
    return jnp.where(c == 0, by_x, by_y)


def call(kernel, outs, scratch, in_specs, out_specs, flops, moved, mib, name):
    return pl.pallas_call(
        kernel,
        out_shape=outs,
        in_specs=in_specs,
        out_specs=out_specs,
        scratch_shapes=scratch,
        compiler_params=pltpu.CompilerParams(vmem_limit_bytes=mib * 2**20),
        cost_estimate=pl.CostEstimate(flops=flops, bytes_accessed=moved, transcendentals=0),
        name=name,
    )


def dot_nt(a, b):
    return lax.dot_general(a, b, (((1,), (1,)), ((), ())), preferred_element_type=F32)


def dot_nn(a, b):
    return jnp.dot(a, b, preferred_element_type=F32)


def shape(dims, kind=BF16):
    return jax.ShapeDtypeStruct(dims, kind)


def column(row):
    return jnp.broadcast_to(row, (128, row.shape[1])).T[:, 0:1]


def row(col):
    return jnp.broadcast_to(col, (col.shape[0], 128)).T[0:1, :]


def dyn(index, size):
    return pl.ds(pl.multiple_of(index * size, size), size)


def run(copies):
    for copy in copies:
        copy.start()
    return copies


def finish(copies):
    for copy in copies:
        copy.wait()


def mask_kernel(base_ref, idx_ref, out_ref):
    chosen, tokens = idx_ref.shape
    n_feat = out_ref.shape[1]
    step = 32
    for part in range(2):
        base = base_ref[part]

        def chunk(i, carry):
            first = pl.multiple_of(i * step, step)
            names = lax.broadcasted_iota(jnp.int32, (step, tokens), 0) + (base + first)
            found = jnp.zeros((step, tokens), F32)
            for k in range(chosen):
                found = jnp.where(idx_ref[pl.ds(k, 1), :] == names, 1.0, found)
            out_ref[part, pl.ds(first, step), :] = found.astype(BF16)
            return carry

        lax.fori_loop(0, n_feat // step, chunk, 0)


def encode_kernel(d1s, first, *refs):
    x_a, x_b, enc_own, enc_other = refs[:4]
    if first:
        bias_refs = refs[4:6]
        acc_out, x_out, xs, weights, sems, w_sems, out_sem = refs[6:]
    else:
        acc_in, mask_ref, act_ref, x_out, xs, weights, sems, w_sems, out_sem = refs[4:]
    c, x, y = place()
    copies = []
    for i, ref in enumerate((x_a, x_b)):
        for d2 in range(4):
            half, jj = tile_in_pair(c, x, d1s, i, d2)
            copies.append(
                pltpu.make_async_copy(
                    ref.at[d2], xs.at[jj, dyn(half, 128), :], sems.at[i * 4 + d2]
                )
            )
    run(copies)
    loads = []
    for part, ref in enumerate((enc_own, enc_other)):
        for jj in range(4):
            j = pair_block(c, x, y, d1s, jj)
            cols = slice(jj * 512, jj * 512 + 512)
            loads.append(
                pltpu.make_async_copy(
                    ref.at[:, dyn(j, 512)], weights.at[part, :, cols], w_sems.at[part * 4 + jj]
                )
            )
    run(loads)
    finish(copies)
    back = pltpu.make_async_copy(xs, x_out, out_sem)
    back.start()
    finish(loads)
    for part in range(2):
        if first:
            total = column(bias_refs[part][...])
        else:
            total = acc_in[part]
        for jj in range(4):
            total = total + dot_nt(weights[part, :, jj * 512 : jj * 512 + 512], xs[jj])
        if first:
            acc_out[part] = total
            continue
        for half in range(2):
            tokens = slice(half * 128, half * 128 + 128)
            chosen = mask_ref[part, :, dyn(half * 2 + c, 128)].astype(F32)
            act_ref[part, :, tokens] = jnp.where(chosen > 0, total[:, tokens], 0.0).astype(BF16)
    back.wait()


def decode_kernel(d1s, half_ref, recv_ref, dec_hbm, dec_other, *refs):
    outs = refs[: 2 * len(d1s)]
    at, dec, blk, sems, out_sems = refs[2 * len(d1s) :]
    c, x, y = place()
    loads, used = [], []
    if len(d1s) == 1:
        for d2 in range(4):
            half, j = tile_at(c, x, y, d1s[0], d2)
            to = slice(d2 * 512, d2 * 512 + 512)
            loads += [
                pltpu.make_async_copy(
                    dec_hbm.at[:, dyn(c * 8 + j, 512)], dec.at[0, :, to], sems.at[0, d2]
                ),
                pltpu.make_async_copy(
                    dec_other.at[:, dyn(j, 512)], dec.at[1, :, to], sems.at[1, d2]
                ),
            ]
    else:
        loads = [
            pltpu.make_async_copy(dec_hbm.at[:, dyn(c, 4096)], dec.at[0], sems.at[0, 0]),
            pltpu.make_async_copy(dec_other, dec.at[1], sems.at[1, 0]),
        ]
    run(loads)
    for part in range(2):
        for half in range(2):
            tokens = slice(half * 128, half * 128 + 128)
            cols = slice(part * 256, part * 256 + 256)
            at[dyn(half * 2 + c, 128), cols] = (
                half_ref[part, :, tokens].astype(F32).T.astype(BF16)
            )
            at[dyn(half * 2 + 1 - c, 128), cols] = (
                recv_ref[1 - part, :, tokens].astype(F32).T.astype(BF16)
            )
    finish(loads)
    copies = []
    for n, d1 in enumerate(d1s):
        for d2 in range(4):
            half, j = tile_at(c, x, y, d1, d2)
            rows = dyn(half, 256)
            cols = slice(d2 * 512, d2 * 512 + 512) if len(d1s) == 1 else dyn(j, 512)
            total = dot_nn(at[rows, 0:256], dec[0, :, cols])
            total += dot_nn(at[rows, 256:512], dec[1, :, cols])
            blk[n, d2 // 2, d2 % 2] = total.astype(BF16)
            if d2 % 2 == 1:
                copies += run(
                    [
                        pltpu.make_async_copy(
                            blk.at[n, d2 // 2], outs[2 * n + d2 // 2], out_sems.at[n, d2 // 2]
                        )
                    ]
                )
    finish(copies)


def backward_kernel(parts, d1s, first, *refs):
    e_refs, refs = (refs[0:2], refs[2:4]), refs[4:]
    half_ref, recv_ref, refs = refs[0], refs[1], refs[2:]
    dec_refs, refs = refs[: len(parts)], refs[len(parts) :]
    if not first:
        d_ins, refs = refs[: len(parts)], refs[len(parts) :]
    d_outs, refs = refs[: len(parts)], refs[len(parts) :]
    g_outs, refs = refs[: len(parts)], refs[len(parts) :]
    err, dec, af, g_blk, sems, w_sems, out_sems = refs
    c, x, y = place()
    copies = []
    for i, pair in enumerate(e_refs):
        for d2 in range(4):
            half, jj = tile_in_pair(c, x, d1s, i, d2)
            copies.append(
                pltpu.make_async_copy(
                    pair[d2 // 2].at[d2 % 2],
                    err.at[jj, dyn(half, 256), :],
                    sems.at[i * 4 + d2],
                )
            )
    run(copies)
    loads = []
    for n, part in enumerate(parts):
        for jj in range(4):
            j = pair_block(c, x, y, d1s, jj)
            block = c * 8 + j if part == 0 else j
            loads.append(
                pltpu.make_async_copy(
                    dec_refs[n].at[:, dyn(block, 512)],
                    dec.at[n, :, jj * 512 : jj * 512 + 512],
                    w_sems.at[n, jj],
                )
            )
    run(loads)
    for n, part in enumerate(parts):
        for half in range(2):
            tokens = slice(half * 128, half * 128 + 128)
            af[n, :, dyn(half * 2 + c, 128)] = half_ref[part, :, tokens]
            af[n, :, dyn(half * 2 + 1 - c, 128)] = recv_ref[1 - part, :, tokens]
    finish(copies)
    finish(loads)
    outs = []
    for n, part in enumerate(parts):
        total = None if first else d_ins[n][:, 0:512]
        square = 0.0 if first else d_ins[n][:, 512:513]
        for jj in range(4):
            cols = slice(jj * 512, jj * 512 + 512)
            g = dot_nn(af[n], err[jj])
            g_blk[n, :, cols] = g.astype(BF16)
            square = square + jnp.sum(g * g, axis=1, keepdims=True)
            outs += run(
                [
                    pltpu.make_async_copy(
                        g_blk.at[n, :, cols], g_outs[n].at[:, cols], out_sems.at[n, jj]
                    )
                ]
            )
            term = dot_nt(dec[n, :, cols], err[jj])
            total = term if total is None else total + term
        d_outs[n][:, 0:512] = total
        d_outs[n][:, 512:640] = jnp.broadcast_to(square, (square.shape[0], 128))
    finish(outs)


def step_kernel(
    d_mine, d_got, mask_ref, xo_a, xo_b, xt_a, xt_b, go_a, go_b, gg_a, gg_b, esec, dsec,
    enc_step, dec_step, enc_new, dec_new,
    xs, gs, genc, d_blk, e_blk, sems, g_sems, d_sems, e_sems,
):
    c, x, y = place()
    width = genc.shape[1]
    pairs = ((0, 2), (1, 3))
    x_loads, g_loads, blocks = [], [], []
    for n, (core, xp, gp) in enumerate(
        ((c, (xo_a, xo_b), (go_a, go_b)), (1 - c, (xt_a, xt_b), (gg_a, gg_b)))
    ):
        for p, d1s in enumerate(pairs):
            g_loads.append(pltpu.make_async_copy(gp[p], gs.at[n, p], g_sems.at[n, p]))
            for jj in range(4):
                j = pair_block(core, x, y, d1s, jj)
                blocks.append((n, p, jj, core, j))
                x_loads.append(
                    pltpu.make_async_copy(
                        xp[p].at[jj], xs.at[n, j], sems.at[n, p * 4 + jj]
                    )
                )
    run(x_loads)
    run(g_loads)
    chosen = mask_ref[0].astype(F32)
    touched = row(jnp.max(chosen, axis=1, keepdims=True)) > 0
    square = row(d_mine[:, 512:513] + d_got[:, 512:513])
    old = dsec[...]
    new = DECAY_RATE * old + (1.0 - DECAY_RATE) * (square / (2 * width))
    v_dec = jnp.where(touched, new, old)
    dec_new[...] = v_dec
    rate_dec = column(jnp.where(touched, -1.0 / (jnp.sqrt(v_dec) + EPSILON), 0.0))
    grad = jnp.where(chosen > 0, d_mine[:, 0:512] + d_got[:, 0:512], 0.0).astype(BF16)
    by_core = [
        jnp.concatenate([grad[:, 0:128], grad[:, 256:384]], 1),
        jnp.concatenate([grad[:, 128:256], grad[:, 384:512]], 1),
    ]
    dact = [
        jnp.where(c == 0, by_core[0], by_core[1]),
        jnp.where(c == 0, by_core[1], by_core[0]),
    ]
    finish(x_loads)
    finish(g_loads)
    outs = []
    total = 0.0
    for j in range(8):
        cols = slice(j * 512, j * 512 + 512)
        g = dot_nn(dact[0], xs[0, j]) + dot_nn(dact[1], xs[1, j])
        genc[:, cols] = g
        total = total + jnp.sum(g * g, axis=1, keepdims=True)
        for n, p, jj, core, block in blocks[2 * j : 2 * j + 2]:
            part = slice(jj * 512, jj * 512 + 512)
            d_blk[n, p, :, part] = (gs[n, p, :, part].astype(F32) * rate_dec).astype(BF16)
            outs += run(
                [
                    pltpu.make_async_copy(
                        d_blk.at[n, p, :, part],
                        dec_step.at[:, dyn(core * 8 + block, 512)],
                        d_sems.at[n, p * 4 + jj],
                    )
                ]
            )
    old = esec[...]
    new = DECAY_RATE * old + (1.0 - DECAY_RATE) * (row(total) / width)
    v_enc = jnp.where(touched, new, old)
    enc_new[...] = v_enc
    rate_enc = column(jnp.where(touched, -1.0 / (jnp.sqrt(v_enc) + EPSILON), 0.0))
    for j in range(4):
        cols = slice(j * 1024, j * 1024 + 1024)
        e_blk[:, cols] = (genc[:, cols] * rate_enc).astype(BF16)
        outs += run(
            [pltpu.make_async_copy(e_blk.at[:, cols], enc_step.at[:, cols], e_sems.at[j])]
        )
    finish(outs)


def body(resid, target, feat_idx, enc_weight, enc_bias, dec_weight, enc_second, dec_second):
    l, z = lax.axis_index("l"), lax.axis_index("z")
    xh, xl, c, y = (lax.axis_index(n) for n in ("xh", "xl", "c", "y"))
    is_one = c == 1
    n_f, width = enc_weight.shape

    digits = jnp.concatenate([feat_idx // 128, feat_idx % 128], 1).astype(BF16)
    packed = jnp.concatenate([resid, digits.reshape(8, 512)], 0)
    by_z = gather(packed, z_get)
    x_z = jnp.concatenate([p[:32] for p in by_z], 0)

    digits = jnp.concatenate([p[32:].reshape(32, 128) for p in by_z], 0)
    digits = digits.astype(jnp.int32)
    idx = digits[:, :64] * 128 + digits[:, 64:]
    other = swap_cores(idx)
    idx = jnp.concatenate([jnp.where(is_one, other, idx), jnp.where(is_one, idx, other)], 0)
    other = lax.ppermute(idx, "xh", [(0, 1), (1, 0)])
    idx = jnp.concatenate([jnp.where(xh == 1, other, idx), jnp.where(xh == 1, idx, other)], 0)
    feat = xl * 4 + y
    member = z * 4 + xh * 2 + c
    mate = z * 4 + xh * 2 + (1 - c)
    bases = jnp.stack([(member * 8 + feat) * n_f, (mate * 8 + feat) * n_f]).astype(jnp.int32)
    mask = call(
        mask_kernel, shape((2, n_f, 512)), [], [SMEM, VMEM], VMEM, 4 * 10**9, 2**20, 4, "mask"
    )(bases, idx.T)

    enc_other = swap_cores(enc_weight)
    bias_other = swap_cores(enc_bias)
    dec_other = swap_cores(lax.dynamic_slice_in_dim(dec_weight, (1 - c) * width, width, 1))
    x_1 = jnp.stack(gather(x_z, lambda v, d: ring_get(v, 2, d)))
    x_blocks = gather(x_1, lambda v, d: ring_get(v, 1, d))

    def encode(d1s, extra, extra_specs, outs, out_specs):
        first = d1s[0] == 0
        return call(
            lambda *refs: encode_kernel(d1s, first, *refs),
            outs + (shape((4, 256, 512)),),
            [
                pltpu.VMEM((4, 256, 512), BF16),
                pltpu.VMEM((2, n_f, 2048), BF16),
                DMA((8,)),
                DMA((8,)),
                DMA,
            ],
            [ANY] * 4 + extra_specs,
            out_specs + (ANY,),
            512 * 256 * width,
            4 * 2**20,
            14,
            "encode_near" if first else "encode_far",
        )(x_blocks[d1s[0]], x_blocks[d1s[1]], enc_weight, enc_other, *extra)

    acc, xo_a = encode(
        (0, 2), (enc_bias[None], bias_other[None]), [VMEM] * 2, (shape((2, n_f, 256), F32),), (VMEM,)
    )
    act_half, xo_b = encode((1, 3), (acc, mask), [VMEM] * 2, (shape((2, n_f, 256)),), (VMEM,))
    act_recv = swap_cores(act_half)

    def decode(d1s):
        wide = 2048 if len(d1s) == 1 else width
        return call(
            lambda *refs: decode_kernel(d1s, *refs),
            (shape((2, 256, 512)),) * (2 * len(d1s)),
            [
                pltpu.VMEM((512, 512), BF16),
                pltpu.VMEM((2, n_f, wide), BF16),
                pltpu.VMEM((len(d1s), 2, 2, 256, 512), BF16),
                DMA((2, 4)),
                DMA((3, 2)),
            ],
            [VMEM, VMEM, ANY, ANY],
            (ANY,) * (2 * len(d1s)),
            2 * 512 * 128 * width * len(d1s),
            4 * 2**20,
            18,
            "decode_far" if len(d1s) == 1 else "decode_near",
        )(act_half, act_recv, dec_weight, dec_other)

    far = decode((2,))
    up_a = ring_put(far[0], 1, 1)
    down_b = ring_put(far[1], 1, 3)
    plus_a, plus_b, minus_a, minus_b, own_a, own_b = decode((1, 3, 0))
    up_b = ring_put(plus_b, 1, 1)
    down_a = ring_put(minus_a, 1, 3)
    next_a = ring_put((plus_a.astype(F32) + up_a.astype(F32)).astype(BF16), 1, 1)
    next_b = ring_put((minus_b.astype(F32) + down_b.astype(F32)).astype(BF16), 1, 3)

    def scatter(parts, put):
        far = put(parts[2].astype(BF16), 2)
        got = [parts[0], put(parts[1].astype(BF16), 1), far, put(parts[3].astype(BF16), 3)]
        return got

    halves = ((own_a, next_a, down_a), (own_b, next_b, up_b))
    parts = [sum(g[d % 2].astype(F32) for g in halves[d // 2]) for d in range(4)]
    got = scatter(parts, lambda v, d: ring_put(v, 2, d))
    sums = sum(g.astype(F32) for g in got).reshape(2, 4, 32, 512)
    got = scatter([sums[:, d] for d in range(4)], lambda v, d: z_get(v, -d))
    total = sum(g.astype(F32) for g in got)

    other = swap_cores(target)
    tgt = jnp.stack([jnp.where(is_one, other, target), jnp.where(is_one, target, other)])
    tgt_next = lax.ppermute(tgt, ("l", "c"), [(2, 1)])
    tgt = jnp.where(is_one, tgt_next, tgt)
    peer = lax.ppermute(total.astype(BF16), ("l", "c"), [(1, 2), (2, 1)])
    err = (total + peer.astype(F32) - tgt.astype(F32)).astype(BF16)
    err = jnp.where((l == 1) & is_one, jnp.zeros_like(err), err)

    err = jnp.stack(gather(err, z_get), 1).reshape(256, 512)
    err = gather(err, lambda v, d: ring_get(v, 2, d))
    err_a, err_b = jnp.stack(err[:2]), jnp.stack(err[2:])
    plus_a = ring_get(err_a, 1, 1)
    minus_b = ring_get(err_b, 1, 3)
    plus_b = ring_get(err_b, 1, 1)
    minus_a = ring_get(err_a, 1, 3)
    far_a = ring_get(plus_a, 1, 1)
    far_b = ring_get(minus_b, 1, 3)
    x_hold = lax.optimization_barrier((xo_a, xo_b, minus_a))
    xt_a = swap_cores(x_hold[0])
    xt_b = swap_cores(x_hold[1])

    def backward(parts, d1s, errs, init):
        first = not init
        weights = [(dec_weight, dec_other)[p] for p in parts]
        n = len(parts)
        outs = call(
            lambda *refs: backward_kernel(parts, d1s, first, *refs),
            (shape((n_f, 640), F32),) * n + (shape((n_f, 2048)),) * n,
            [
                pltpu.VMEM((4, 512, 512), BF16),
                pltpu.VMEM((n, n_f, 2048), BF16),
                pltpu.VMEM((n, n_f, 512), BF16),
                pltpu.VMEM((n, n_f, 2048), BF16),
                DMA((8,)),
                DMA((n, 4)),
                DMA((n, 4)),
            ],
            [ANY] * 4 + [VMEM] * 2 + [ANY] * n + [VMEM] * len(init),
            (VMEM,) * n + (ANY,) * n,
            2 * n * 512 * 256 * width,
            (2 + 2 * n) * 2**20,
            20,
            "backward_" + "_".join(str(p) for p in parts),
        )(*errs, act_half, act_recv, *weights, *init)
        return outs

    d_own, d_other, go_b, gt_b = backward((0, 1), (1, 3), (plus_a, plus_b, minus_a, minus_b), ())
    gg_b = swap_cores(gt_b)
    near = (err_a, err_b, far_a, far_b)
    d_other, gt_a = backward((1,), (0, 2), near, (d_other,))
    d_got = swap_cores(d_other)
    gg_a = swap_cores(gt_a)
    d_own, go_a = backward((0,), (0, 2), near, (d_own,))
    enc_step, dec_step, enc_new, dec_new = call(
        step_kernel,
        (
            shape((n_f, width)), shape((n_f, 2 * width)),
            shape((1, n_f), F32), shape((1, n_f), F32),
        ),
        [
            pltpu.VMEM((2, 8, 256, 512), BF16),
            pltpu.VMEM((2, 2, n_f, 2048), BF16),
            pltpu.VMEM((n_f, width), F32),
            pltpu.VMEM((2, 2, n_f, 2048), BF16),
            pltpu.VMEM((n_f, width), BF16),
            DMA((2, 8)),
            DMA((2, 2)),
            DMA((2, 8)),
            DMA((4,)),
        ],
        [VMEM] * 3 + [ANY] * 8 + [VMEM] * 2,
        (ANY, ANY, VMEM, VMEM),
        2 * 512 * 256 * width,
        14 * 2**20,
        34,
        "steps",
    )(
        d_own, d_got, mask, xo_a, xo_b, xt_a, xt_b, go_a, go_b, gg_a, gg_b,
        enc_second[None], dec_second[None],
    )
    return enc_step, dec_step, enc_new.reshape(n_f), dec_new.reshape(n_f)


def solution(mesh):
    devices = mesh.devices.reshape(2, 4, 2, 2, 2, 4)
    fine = Mesh(devices, ("l", "z", "xh", "c", "xl", "y"))
    rows, cols = ("l", "z", "xh", "c"), ("xl", "y")
    in_specs = (
        P(rows, cols),
        P(rows, cols),
        P(rows, None),
        P(rows + cols, None),
        P(rows + cols),
        P(rows + cols, None),
        P(rows + cols),
        P(rows + cols),
    )
    out_specs = (P(rows + cols, None), P(rows + cols, None), P(rows + cols), P(rows + cols))
    return jax.shard_map(body, mesh=fine, in_specs=in_specs, out_specs=out_specs, check_vma=False)
```

```python
import jax
import jax.numpy as jnp
from jax import lax
from jax.experimental import pallas as pl
from jax.experimental.pallas import tpu as pltpu
from jax.sharding import Mesh, PartitionSpec as P

EPSILON = 1e-08
DECAY_RATE = 0.99
F32 = jnp.float32
BF16 = jnp.bfloat16
ANY = pl.BlockSpec(memory_space=pl.ANY)
VMEM = pl.BlockSpec(memory_space=pltpu.VMEM)
SMEM = pl.BlockSpec(memory_space=pltpu.SMEM)
DMA = pltpu.SemaphoreType.DMA
PLANE = ("xh", "c", "xl", "y")


def ring_ahead(which, steps):
    ahead = []
    for place in range(32):
        xh, c, xl, y = place // 16, place // 8 % 2, place // 4 % 2, place % 4
        x = xh * 2 + xl
        if (which == 1) == (c == 0):
            x = (x + steps) % 4
        else:
            y = (y + steps) % 4
        ahead.append(((x // 2) * 2 + c) * 8 + (x % 2) * 4 + y)
    return ahead


def ring_get(value, which, steps):
    ahead = ring_ahead(which, steps)
    return lax.ppermute(value, PLANE, [(ahead[i], i) for i in range(32)])


def ring_put(value, which, steps):
    return ring_get(value, which, -steps)


def z_get(value, steps):
    return lax.ppermute(value, "z", [((i + steps) % 4, i) for i in range(4)])


def swap_cores(value):
    return lax.ppermute(value, "c", [(0, 1), (1, 0)])


def gather(value, get):
    far = get(value, 2)
    return [value, get(value, 1), far, get(value, 3)]


def place():
    x = lax.axis_index("xh") * 2 + lax.axis_index("xl")
    return lax.axis_index("c"), x, lax.axis_index("y")


def tile_at(c, x, y, d1, d2):
    tx = (x + jnp.where(c == 0, d1, d2)) % 4
    ty = (y + jnp.where(c == 0, d2, d1)) % 4
    return tx // 2, (tx % 2) * 4 + ty


def tile_in_pair(c, x, d1s, i, d2):
    tx = (x + jnp.where(c == 0, d1s[i], d2)) % 4
    return tx // 2, jnp.where(c == 0, d2, i * 2 + tx % 2)


def pair_block(c, x, y, d1s, jj):
    by_x = ((x + d1s[0]) % 2) * 4 + (y + jj) % 4
    by_y = (jj % 2) * 4 + (y + d1s[jj // 2]) % 4
    return jnp.where(c == 0, by_x, by_y)


def call(kernel, outs, scratch, in_specs, out_specs, flops, moved, mib, name):
    return pl.pallas_call(
        kernel,
        out_shape=outs,
        in_specs=in_specs,
        out_specs=out_specs,
        scratch_shapes=scratch,
        compiler_params=pltpu.CompilerParams(vmem_limit_bytes=mib * 2**20),
        cost_estimate=pl.CostEstimate(flops=flops, bytes_accessed=moved, transcendentals=0),
        name=name,
    )


def dot_nt(a, b):
    return lax.dot_general(a, b, (((1,), (1,)), ((), ())), preferred_element_type=F32)


def dot_nn(a, b):
    return jnp.dot(a, b, preferred_element_type=F32)


def shape(dims, kind=BF16):
    return jax.ShapeDtypeStruct(dims, kind)


def column(row):
    return jnp.broadcast_to(row, (128, row.shape[1])).T[:, 0:1]


def row(col):
    return jnp.broadcast_to(col, (col.shape[0], 128)).T[0:1, :]


def dyn(index, size):
    return pl.ds(pl.multiple_of(index * size, size), size)


def run(copies):
    for copy in copies:
        copy.start()
    return copies


def finish(copies):
    for copy in copies:
        copy.wait()


def mask_kernel(base_ref, idx_ref, out_ref):
    chosen, tokens = idx_ref.shape
    n_feat = out_ref.shape[1]
    step = 32
    for part in range(2):
        base = base_ref[part]

        def chunk(i, carry):
            first = pl.multiple_of(i * step, step)
            names = lax.broadcasted_iota(jnp.int32, (step, tokens), 0) + (base + first)
            found = jnp.zeros((step, tokens), F32)
            for k in range(chosen):
                found = jnp.where(idx_ref[pl.ds(k, 1), :] == names, 1.0, found)
            out_ref[part, pl.ds(first, step), :] = found.astype(BF16)
            return carry

        lax.fori_loop(0, n_feat // step, chunk, 0)


def encode_kernel(d1s, first, *refs):
    x_a, x_b, enc_own, enc_other = refs[:4]
    if first:
        bias_refs = refs[4:6]
        acc_out, xs, weights, sems, w_sems = refs[6:]
    else:
        acc_in, mask_ref, near_a, near_b = refs[4:8]
        act_ref, x_out, xs, weights, sems, w_sems, out_sems = refs[8:]
    c, x, y = place()
    copies, outs = [], []
    if not first:
        for i, ref in enumerate((near_a, near_b)):
            for d2 in range(4):
                half, jj = tile_in_pair(c, x, (0, 2), i, d2)
                outs.append(
                    pltpu.make_async_copy(
                        ref.at[d2], x_out.at[0, jj, dyn(half, 128), :], out_sems.at[i * 4 + d2]
                    )
                )
    for i, ref in enumerate((x_a, x_b)):
        for d2 in range(4):
            half, jj = tile_in_pair(c, x, d1s, i, d2)
            copies.append(
                pltpu.make_async_copy(
                    ref.at[d2], xs.at[jj, dyn(half, 128), :], sems.at[i * 4 + d2]
                )
            )
    run(copies)
    loads = []
    for part, ref in enumerate((enc_own, enc_other)):
        for jj in range(4):
            j = pair_block(c, x, y, d1s, jj)
            cols = slice(jj * 512, jj * 512 + 512)
            loads.append(
                pltpu.make_async_copy(
                    ref.at[:, dyn(j, 512)], weights.at[part, :, cols], w_sems.at[part * 4 + jj]
                )
            )
    run(loads)
    finish(copies)
    if not first:
        outs.append(pltpu.make_async_copy(xs, x_out.at[1], out_sems.at[8]))
        run(outs)
    finish(loads)
    for part in range(2):
        if first:
            total = column(bias_refs[part][...])
        else:
            total = acc_in[part]
        for jj in range(4):
            total = total + dot_nt(weights[part, :, jj * 512 : jj * 512 + 512], xs[jj])
        if first:
            acc_out[part] = total
            continue
        for half in range(2):
            tokens = slice(half * 128, half * 128 + 128)
            chosen = mask_ref[part, :, dyn(half * 2 + c, 128)].astype(F32)
            act_ref[part, :, tokens] = jnp.where(chosen > 0, total[:, tokens], 0.0).astype(BF16)
    finish(outs)


def decode_kernel(d1s, half_ref, recv_ref, dec_hbm, dec_other, *refs):
    outs, refs = refs[: 2 * len(d1s)], refs[2 * len(d1s) :]
    if len(d1s) > 1:
        dec_out, refs = refs[0], refs[1:]
    at, dec, blk, sems, out_sems = refs
    c, x, y = place()
    loads, used = [], []
    if len(d1s) == 1:
        for d2 in range(4):
            half, j = tile_at(c, x, y, d1s[0], d2)
            to = slice(d2 * 512, d2 * 512 + 512)
            loads += [
                pltpu.make_async_copy(
                    dec_hbm.at[:, dyn(c * 8 + j, 512)], dec.at[0, :, to], sems.at[0, d2]
                ),
                pltpu.make_async_copy(
                    dec_other.at[:, dyn(j, 512)], dec.at[1, :, to], sems.at[1, d2]
                ),
            ]
    else:
        loads = [
            pltpu.make_async_copy(dec_hbm.at[:, dyn(c, 4096)], dec.at[0], sems.at[0, 0]),
            pltpu.make_async_copy(dec_other, dec.at[1], sems.at[1, 0]),
        ]
    run(loads)
    for part in range(2):
        for half in range(2):
            tokens = slice(half * 128, half * 128 + 128)
            cols = slice(part * 256, part * 256 + 256)
            at[dyn(half * 2 + c, 128), cols] = (
                half_ref[part, :, tokens].astype(F32).T.astype(BF16)
            )
            at[dyn(half * 2 + 1 - c, 128), cols] = (
                recv_ref[1 - part, :, tokens].astype(F32).T.astype(BF16)
            )
    finish(loads)
    copies = []
    if len(d1s) > 1:
        copies += run([pltpu.make_async_copy(dec.at[0], dec_out, out_sems.at[3, 0])])
    for n, d1 in enumerate(d1s):
        for d2 in range(4):
            half, j = tile_at(c, x, y, d1, d2)
            rows = dyn(half, 256)
            cols = slice(d2 * 512, d2 * 512 + 512) if len(d1s) == 1 else dyn(j, 512)
            total = dot_nn(at[rows, 0:256], dec[0, :, cols])
            total += dot_nn(at[rows, 256:512], dec[1, :, cols])
            blk[n, d2 // 2, d2 % 2] = total.astype(BF16)
            if d2 % 2 == 1:
                copies += run(
                    [
                        pltpu.make_async_copy(
                            blk.at[n, d2 // 2], outs[2 * n + d2 // 2], out_sems.at[n, d2 // 2]
                        )
                    ]
                )
    finish(copies)


def backward_kernel(parts, d1s, first, *refs):
    e_refs, refs = (refs[0:2], refs[2:4]), refs[4:]
    half_ref, recv_ref, refs = refs[0], refs[1], refs[2:]
    dec_refs, refs = refs[: len(parts)], refs[len(parts) :]
    if not first:
        d_ins, refs = refs[: len(parts)], refs[len(parts) :]
    d_outs, refs = refs[: len(parts)], refs[len(parts) :]
    g_outs, refs = refs[: len(parts)], refs[len(parts) :]
    err, dec, af, g_blk, sems, w_sems, out_sems = refs
    c, x, y = place()
    copies = []
    for i, pair in enumerate(e_refs):
        for d2 in range(4):
            half, jj = tile_in_pair(c, x, d1s, i, d2)
            copies.append(
                pltpu.make_async_copy(
                    pair[d2 // 2].at[d2 % 2],
                    err.at[jj, dyn(half, 256), :],
                    sems.at[i * 4 + d2],
                )
            )
    run(copies)
    loads = []
    for n, part in enumerate(parts):
        for jj in range(4):
            j = pair_block(c, x, y, d1s, jj)
            loads.append(
                pltpu.make_async_copy(
                    dec_refs[n].at[:, dyn(j, 512)],
                    dec.at[n, :, jj * 512 : jj * 512 + 512],
                    w_sems.at[n, jj],
                )
            )
    run(loads)
    for n, part in enumerate(parts):
        for half in range(2):
            tokens = slice(half * 128, half * 128 + 128)
            af[n, :, dyn(half * 2 + c, 128)] = half_ref[part, :, tokens]
            af[n, :, dyn(half * 2 + 1 - c, 128)] = recv_ref[1 - part, :, tokens]
    finish(copies)
    finish(loads)
    outs = []
    for n, part in enumerate(parts):
        total = None if first else d_ins[n][:, 0:512]
        square = 0.0 if first else d_ins[n][:, 512:513]
        for jj in range(4):
            cols = slice(jj * 512, jj * 512 + 512)
            g = dot_nn(af[n], err[jj])
            g_blk[n, :, cols] = g.astype(BF16)
            square = square + jnp.sum(g * g, axis=1, keepdims=True)
            outs += run(
                [
                    pltpu.make_async_copy(
                        g_blk.at[n, :, cols], g_outs[n].at[:, cols], out_sems.at[n, jj]
                    )
                ]
            )
            term = dot_nt(dec[n, :, cols], err[jj])
            total = term if total is None else total + term
        d_outs[n][:, 0:512] = total
        d_outs[n][:, 512:640] = jnp.broadcast_to(square, (square.shape[0], 128))
    finish(outs)


def step_kernel(
    d_mine, d_got, mask_ref, x_own, x_other, go_a, go_b, gg_a, gg_b, esec, dsec,
    enc_step, dec_step, enc_new, dec_new,
    xs, gs, genc, d_blk, e_blk, sems, g_sems, d_sems, e_sems,
):
    c, x, y = place()
    width = genc.shape[1]
    pairs = ((0, 2), (1, 3))
    x_loads, g_loads, blocks = [], [], []
    for n, (core, xp, gp) in enumerate(
        ((c, x_own, (go_a, go_b)), (1 - c, x_other, (gg_a, gg_b)))
    ):
        for p, d1s in enumerate(pairs):
            g_loads.append(pltpu.make_async_copy(gp[p], gs.at[n, p], g_sems.at[n, p]))
            for jj in range(4):
                j = pair_block(core, x, y, d1s, jj)
                blocks.append((n, p, jj, core, j))
                x_loads.append(
                    pltpu.make_async_copy(
                        xp.at[p, jj], xs.at[n, j], sems.at[n, p * 4 + jj]
                    )
                )
    run(x_loads)
    run(g_loads)
    chosen = mask_ref[0].astype(F32)
    touched = row(jnp.max(chosen, axis=1, keepdims=True)) > 0
    square = row(d_mine[:, 512:513] + d_got[:, 512:513])
    old = dsec[...]
    new = DECAY_RATE * old + (1.0 - DECAY_RATE) * (square / (2 * width))
    v_dec = jnp.where(touched, new, old)
    dec_new[...] = v_dec
    rate_dec = column(jnp.where(touched, -1.0 / (jnp.sqrt(v_dec) + EPSILON), 0.0))
    grad = jnp.where(chosen > 0, d_mine[:, 0:512] + d_got[:, 0:512], 0.0).astype(BF16)
    by_core = [
        jnp.concatenate([grad[:, 0:128], grad[:, 256:384]], 1),
        jnp.concatenate([grad[:, 128:256], grad[:, 384:512]], 1),
    ]
    dact = [
        jnp.where(c == 0, by_core[0], by_core[1]),
        jnp.where(c == 0, by_core[1], by_core[0]),
    ]
    finish(x_loads)
    finish(g_loads)
    outs = []
    total = 0.0
    for j in range(8):
        cols = slice(j * 512, j * 512 + 512)
        g = dot_nn(dact[0], xs[0, j]) + dot_nn(dact[1], xs[1, j])
        genc[:, cols] = g
        total = total + jnp.sum(g * g, axis=1, keepdims=True)
        for n, p, jj, core, block in blocks[2 * j : 2 * j + 2]:
            part = slice(jj * 512, jj * 512 + 512)
            d_blk[n, p, :, part] = (gs[n, p, :, part].astype(F32) * rate_dec).astype(BF16)
            outs += run(
                [
                    pltpu.make_async_copy(
                        d_blk.at[n, p, :, part],
                        dec_step.at[:, dyn(core * 8 + block, 512)],
                        d_sems.at[n, p * 4 + jj],
                    )
                ]
            )
    old = esec[...]
    new = DECAY_RATE * old + (1.0 - DECAY_RATE) * (row(total) / width)
    v_enc = jnp.where(touched, new, old)
    enc_new[...] = v_enc
    rate_enc = column(jnp.where(touched, -1.0 / (jnp.sqrt(v_enc) + EPSILON), 0.0))
    for j in range(4):
        cols = slice(j * 1024, j * 1024 + 1024)
        e_blk[:, cols] = (genc[:, cols] * rate_enc).astype(BF16)
        outs += run(
            [pltpu.make_async_copy(e_blk.at[:, cols], enc_step.at[:, cols], e_sems.at[j])]
        )
    finish(outs)


def body(resid, target, feat_idx, enc_weight, enc_bias, dec_weight, enc_second, dec_second):
    l, z = lax.axis_index("l"), lax.axis_index("z")
    xh, xl, c, y = (lax.axis_index(n) for n in ("xh", "xl", "c", "y"))
    is_one = c == 1
    n_f, width = enc_weight.shape

    digits = jnp.concatenate([feat_idx // 128, feat_idx % 128], 1).astype(BF16)
    packed = jnp.concatenate([resid, digits.reshape(8, 512)], 0)
    by_z = gather(packed, z_get)
    x_z = jnp.concatenate([p[:32] for p in by_z], 0)

    digits = jnp.concatenate([p[32:].reshape(32, 128) for p in by_z], 0)
    digits = digits.astype(jnp.int32)
    idx = digits[:, :64] * 128 + digits[:, 64:]
    other = swap_cores(idx)
    idx = jnp.concatenate([jnp.where(is_one, other, idx), jnp.where(is_one, idx, other)], 0)
    other = lax.ppermute(idx, "xh", [(0, 1), (1, 0)])
    idx = jnp.concatenate([jnp.where(xh == 1, other, idx), jnp.where(xh == 1, idx, other)], 0)
    feat = xl * 4 + y
    member = z * 4 + xh * 2 + c
    mate = z * 4 + xh * 2 + (1 - c)
    bases = jnp.stack([(member * 8 + feat) * n_f, (mate * 8 + feat) * n_f]).astype(jnp.int32)
    mask = call(
        mask_kernel, shape((2, n_f, 512)), [], [SMEM, VMEM], VMEM, 4 * 10**9, 2**20, 4, "mask"
    )(bases, idx.T)

    enc_other = swap_cores(enc_weight)
    bias_other = swap_cores(enc_bias)
    dec_other = swap_cores(lax.dynamic_slice_in_dim(dec_weight, (1 - c) * width, width, 1))
    x_1 = jnp.stack(gather(x_z, lambda v, d: ring_get(v, 2, d)))
    x_blocks = gather(x_1, lambda v, d: ring_get(v, 1, d))

    def encode(d1s, extra, extra_specs, outs, out_specs, sems):
        first = d1s[0] == 0
        return call(
            lambda *refs: encode_kernel(d1s, first, *refs),
            outs,
            [
                pltpu.VMEM((4, 256, 512), BF16),
                pltpu.VMEM((2, n_f, 2048), BF16),
                DMA((8,)),
                DMA((8,)),
            ]
            + sems,
            [ANY] * 4 + extra_specs,
            out_specs,
            512 * 256 * width,
            4 * 2**20,
            14,
            "encode_near" if first else "encode_far",
        )(x_blocks[d1s[0]], x_blocks[d1s[1]], enc_weight, enc_other, *extra)

    acc = encode(
        (0, 2), (enc_bias[None], bias_other[None]), [VMEM] * 2, shape((2, n_f, 256), F32), VMEM, []
    )
    act_half, x_own = encode(
        (1, 3),
        (acc, mask, x_blocks[0], x_blocks[2]),
        [VMEM, VMEM, ANY, ANY],
        (shape((2, n_f, 256)), shape((2, 4, 256, 512))),
        (VMEM, ANY),
        [DMA((9,))],
    )
    act_recv = swap_cores(act_half)
    x_own, act_recv = lax.optimization_barrier((x_own, act_recv))
    x_other = swap_cores(x_own)

    def decode(d1s):
        wide, extra = (2048, ()) if len(d1s) == 1 else (width, (shape((n_f, width)),))
        return call(
            lambda *refs: decode_kernel(d1s, *refs),
            (shape((2, 256, 512)),) * (2 * len(d1s)) + extra,
            [
                pltpu.VMEM((512, 512), BF16),
                pltpu.VMEM((2, n_f, wide), BF16),
                pltpu.VMEM((len(d1s), 2, 2, 256, 512), BF16),
                DMA((2, 4)),
                DMA((4, 2)),
            ],
            [VMEM, VMEM, ANY, ANY],
            (ANY,) * (2 * len(d1s) + len(extra)),
            2 * 512 * 128 * width * len(d1s),
            4 * 2**20,
            18,
            "decode_far" if len(d1s) == 1 else "decode_near",
        )(act_half, act_recv, dec_weight, dec_other)

    far = decode((2,))
    up_a = ring_put(far[0], 1, 1)
    down_b = ring_put(far[1], 1, 3)
    plus_a, plus_b, minus_a, minus_b, own_a, own_b, dec_own = decode((1, 3, 0))
    own_a, x_other = lax.optimization_barrier((own_a, x_other))
    up_b = ring_put(plus_b, 1, 1)
    down_a = ring_put(minus_a, 1, 3)
    next_a = ring_put((plus_a.astype(F32) + up_a.astype(F32)).astype(BF16), 1, 1)
    next_b = ring_put((minus_b.astype(F32) + down_b.astype(F32)).astype(BF16), 1, 3)

    def scatter(parts, put):
        far = put(parts[2].astype(BF16), 2)
        got = [parts[0], put(parts[1].astype(BF16), 1), far, put(parts[3].astype(BF16), 3)]
        return got

    halves = ((own_a, next_a, down_a), (own_b, next_b, up_b))
    parts = [sum(g[d % 2].astype(F32) for g in halves[d // 2]) for d in range(4)]
    got = scatter(parts, lambda v, d: ring_put(v, 2, d))
    sums = sum(g.astype(F32) for g in got).reshape(2, 4, 32, 512)
    got = scatter([sums[:, d] for d in range(4)], lambda v, d: z_get(v, -d))
    total = sum(g.astype(F32) for g in got)

    other = swap_cores(target)
    tgt = jnp.stack([jnp.where(is_one, other, target), jnp.where(is_one, target, other)])
    tgt_next = lax.ppermute(tgt, ("l", "c"), [(2, 1)])
    tgt = jnp.where(is_one, tgt_next, tgt)
    peer = lax.ppermute(total.astype(BF16), ("l", "c"), [(1, 2), (2, 1)])
    err = (total + peer.astype(F32) - tgt.astype(F32)).astype(BF16)
    err = jnp.where((l == 1) & is_one, jnp.zeros_like(err), err)

    err = jnp.stack(gather(err, z_get), 1).reshape(256, 512)
    err = gather(err, lambda v, d: ring_get(v, 2, d))
    err_a, err_b = jnp.stack(err[:2]), jnp.stack(err[2:])
    plus_a = ring_get(err_a, 1, 1)
    minus_b = ring_get(err_b, 1, 3)
    plus_b = ring_get(err_b, 1, 1)
    minus_a = ring_get(err_a, 1, 3)
    far_a = ring_get(plus_a, 1, 1)
    far_b = ring_get(minus_b, 1, 3)

    def backward(parts, d1s, errs, init):
        first = not init
        weights = [(dec_own, dec_other)[p] for p in parts]
        n = len(parts)
        outs = call(
            lambda *refs: backward_kernel(parts, d1s, first, *refs),
            (shape((n_f, 640), F32),) * n + (shape((n_f, 2048)),) * n,
            [
                pltpu.VMEM((4, 512, 512), BF16),
                pltpu.VMEM((n, n_f, 2048), BF16),
                pltpu.VMEM((n, n_f, 512), BF16),
                pltpu.VMEM((n, n_f, 2048), BF16),
                DMA((8,)),
                DMA((n, 4)),
                DMA((n, 4)),
            ],
            [ANY] * 4 + [VMEM] * 2 + [ANY] * n + [VMEM] * len(init),
            (VMEM,) * n + (ANY,) * n,
            2 * n * 512 * 256 * width,
            (2 + 2 * n) * 2**20,
            20,
            "backward_" + "_".join(str(p) for p in parts),
        )(*errs, act_half, act_recv, *weights, *init)
        return outs

    d_own, d_other, go_b, gt_b = backward((0, 1), (1, 3), (plus_a, plus_b, minus_a, minus_b), ())
    gg_b = swap_cores(gt_b)
    near = (err_a, err_b, far_a, far_b)
    d_other, gt_a = backward((1,), (0, 2), near, (d_other,))
    d_got = swap_cores(d_other)
    gg_a = swap_cores(gt_a)
    d_own, go_a = backward((0,), (0, 2), near, (d_own,))
    enc_step, dec_step, enc_new, dec_new = call(
        step_kernel,
        (
            shape((n_f, width)), shape((n_f, 2 * width)),
            shape((1, n_f), F32), shape((1, n_f), F32),
        ),
        [
            pltpu.VMEM((2, 8, 256, 512), BF16),
            pltpu.VMEM((2, 2, n_f, 2048), BF16),
            pltpu.VMEM((n_f, width), F32),
            pltpu.VMEM((2, 2, n_f, 2048), BF16),
            pltpu.VMEM((n_f, width), BF16),
            DMA((2, 8)),
            DMA((2, 2)),
            DMA((2, 8)),
            DMA((4,)),
        ],
        [VMEM] * 3 + [ANY] * 6 + [VMEM] * 2,
        (ANY, ANY, VMEM, VMEM),
        2 * 512 * 256 * width,
        14 * 2**20,
        34,
        "steps",
    )(
        d_own, d_got, mask, x_own, x_other, go_a, go_b, gg_a, gg_b,
        enc_second[None], dec_second[None],
    )
    return enc_step, dec_step, enc_new.reshape(n_f), dec_new.reshape(n_f)


def solution(mesh):
    devices = mesh.devices.reshape(2, 4, 2, 2, 2, 4)
    fine = Mesh(devices, ("l", "z", "xh", "c", "xl", "y"))
    rows, cols = ("l", "z", "xh", "c"), ("xl", "y")
    in_specs = (
        P(rows, cols),
        P(rows, cols),
        P(rows, None),
        P(rows + cols, None),
        P(rows + cols),
        P(rows + cols, None),
        P(rows + cols),
        P(rows + cols),
    )
    out_specs = (P(rows + cols, None), P(rows + cols, None), P(rows + cols), P(rows + cols))
    return jax.shard_map(body, mesh=fine, in_specs=in_specs, out_specs=out_specs, check_vma=False)
```

```python
import jax
import jax.numpy as jnp
from jax import lax
from jax.experimental import pallas as pl
from jax.experimental.pallas import tpu as pltpu
from jax.sharding import Mesh, PartitionSpec as P

EPSILON = 1e-08
DECAY_RATE = 0.99
F32 = jnp.float32
BF16 = jnp.bfloat16
ANY = pl.BlockSpec(memory_space=pl.ANY)
VMEM = pl.BlockSpec(memory_space=pltpu.VMEM)
SMEM = pl.BlockSpec(memory_space=pltpu.SMEM)
DMA = pltpu.SemaphoreType.DMA
PLANE = ("xh", "c", "xl", "y")


def ring_ahead(which, steps):
    ahead = []
    for place in range(32):
        xh, c, xl, y = place // 16, place // 8 % 2, place // 4 % 2, place % 4
        x = xh * 2 + xl
        if (which == 1) == (c == 0):
            x = (x + steps) % 4
        else:
            y = (y + steps) % 4
        ahead.append(((x // 2) * 2 + c) * 8 + (x % 2) * 4 + y)
    return ahead


def ring_get(value, which, steps):
    ahead = ring_ahead(which, steps)
    return lax.ppermute(value, PLANE, [(ahead[i], i) for i in range(32)])


def ring_put(value, which, steps):
    return ring_get(value, which, -steps)


def z_get(value, steps):
    return lax.ppermute(value, "z", [((i + steps) % 4, i) for i in range(4)])


def swap_cores(value):
    return lax.ppermute(value, "c", [(0, 1), (1, 0)])


def gather(value, get):
    far = get(value, 2)
    return [value, get(value, 1), far, get(value, 3)]


def place():
    x = lax.axis_index("xh") * 2 + lax.axis_index("xl")
    return lax.axis_index("c"), x, lax.axis_index("y")


def slot_of(core):
    return jnp.where(lax.axis_index("l") == 0, core, 1 - core)


def tile_at(c, x, y, d1, d2):
    tx = (x + jnp.where(c == 0, d1, d2)) % 4
    ty = (y + jnp.where(c == 0, d2, d1)) % 4
    return tx // 2, (tx % 2) * 4 + ty


def tile_in_pair(c, x, d1s, i, d2):
    tx = (x + jnp.where(c == 0, d1s[i], d2)) % 4
    return tx // 2, jnp.where(c == 0, d2, i * 2 + tx % 2)


def pair_block(c, x, y, d1s, jj):
    by_x = ((x + d1s[0]) % 2) * 4 + (y + jj) % 4
    by_y = (jj % 2) * 4 + (y + d1s[jj // 2]) % 4
    return jnp.where(c == 0, by_x, by_y)


def call(kernel, outs, scratch, in_specs, out_specs, flops, moved, mib, name):
    return pl.pallas_call(
        kernel,
        out_shape=outs,
        in_specs=in_specs,
        out_specs=out_specs,
        scratch_shapes=scratch,
        compiler_params=pltpu.CompilerParams(vmem_limit_bytes=mib * 2**20),
        cost_estimate=pl.CostEstimate(flops=flops, bytes_accessed=moved, transcendentals=0),
        name=name,
    )


def dot_nt(a, b):
    return lax.dot_general(a, b, (((1,), (1,)), ((), ())), preferred_element_type=F32)


def dot_nn(a, b):
    return jnp.dot(a, b, preferred_element_type=F32)


def shape(dims, kind=BF16):
    return jax.ShapeDtypeStruct(dims, kind)


def column(row):
    return jnp.broadcast_to(row, (128, row.shape[1])).T[:, 0:1]


def row(col):
    return jnp.broadcast_to(col, (col.shape[0], 128)).T[0:1, :]


def dyn(index, size):
    return pl.ds(pl.multiple_of(index * size, size), size)


def run(copies):
    for copy in copies:
        copy.start()
    return copies


def finish(copies):
    for copy in copies:
        copy.wait()


def mask_kernel(base_ref, idx_ref, out_ref):
    chosen, tokens = idx_ref.shape
    n_feat = out_ref.shape[1]
    step = 32
    for part in range(2):
        base = base_ref[part]

        def chunk(i, carry):
            first = pl.multiple_of(i * step, step)
            names = lax.broadcasted_iota(jnp.int32, (step, tokens), 0) + (base + first)
            found = jnp.zeros((step, tokens), F32)
            for k in range(chosen):
                found = jnp.where(idx_ref[pl.ds(k, 1), :] == names, 1.0, found)
            out_ref[part, pl.ds(first, step), :] = found.astype(BF16)
            return carry

        lax.fori_loop(0, n_feat // step, chunk, 0)


def encode_kernel(d1s, first, *refs):
    x_a, x_b, enc_own, enc_other = refs[:4]
    if first:
        bias_refs = refs[4:6]
        acc_out, xs, weights, sems, w_sems = refs[6:]
    else:
        acc_in, mask_ref, near_a, near_b = refs[4:8]
        act_ref, x_out, xs, weights, sems, w_sems, out_sems = refs[8:]
    c, x, y = place()
    copies, outs = [], []
    if not first:
        for i, ref in enumerate((near_a, near_b)):
            for d2 in range(4):
                half, jj = tile_in_pair(c, x, (0, 2), i, d2)
                outs.append(
                    pltpu.make_async_copy(
                        ref.at[d2], x_out.at[0, jj, dyn(half, 128), :], out_sems.at[i * 4 + d2]
                    )
                )
    for i, ref in enumerate((x_a, x_b)):
        for d2 in range(4):
            half, jj = tile_in_pair(c, x, d1s, i, d2)
            copies.append(
                pltpu.make_async_copy(
                    ref.at[d2], xs.at[jj, dyn(half, 128), :], sems.at[i * 4 + d2]
                )
            )
    run(copies)
    loads = []
    for part, ref in enumerate((enc_own, enc_other)):
        for jj in range(4):
            j = pair_block(c, x, y, d1s, jj)
            cols = slice(jj * 512, jj * 512 + 512)
            loads.append(
                pltpu.make_async_copy(
                    ref.at[:, dyn(j, 512)], weights.at[part, :, cols], w_sems.at[part * 4 + jj]
                )
            )
    run(loads)
    finish(copies)
    if not first:
        outs.append(pltpu.make_async_copy(xs, x_out.at[1], out_sems.at[8]))
        run(outs)
    finish(loads)
    for part in range(2):
        if first:
            total = column(bias_refs[part][...])
        else:
            total = acc_in[part]
        for jj in range(4):
            total = total + dot_nt(weights[part, :, jj * 512 : jj * 512 + 512], xs[jj])
        if first:
            acc_out[part] = total
            continue
        for half in range(2):
            tokens = slice(half * 128, half * 128 + 128)
            chosen = mask_ref[part, :, dyn(half * 2 + c, 128)].astype(F32)
            act_ref[part, :, tokens] = jnp.where(chosen > 0, total[:, tokens], 0.0).astype(BF16)
    finish(outs)


def decode_kernel(d1s, half_ref, recv_ref, dec_hbm, dec_other, *refs):
    outs, refs = refs[: 2 * len(d1s)], refs[2 * len(d1s) :]
    if len(d1s) > 1:
        dec_out, refs = refs[0], refs[1:]
    at, dec, blk, sems, out_sems = refs
    c, x, y = place()
    loads, used = [], []
    if len(d1s) == 1:
        for d2 in range(4):
            half, j = tile_at(c, x, y, d1s[0], d2)
            to = slice(d2 * 512, d2 * 512 + 512)
            loads += [
                pltpu.make_async_copy(
                    dec_hbm.at[:, dyn(slot_of(c) * 8 + j, 512)],
                    dec.at[0, :, to],
                    sems.at[0, d2],
                ),
                pltpu.make_async_copy(
                    dec_other.at[:, dyn(j, 512)], dec.at[1, :, to], sems.at[1, d2]
                ),
            ]
    else:
        loads = [
            pltpu.make_async_copy(dec_hbm.at[:, dyn(slot_of(c), 4096)], dec.at[0], sems.at[0, 0]),
            pltpu.make_async_copy(dec_other, dec.at[1], sems.at[1, 0]),
        ]
    run(loads)
    for part in range(2):
        for half in range(2):
            tokens = slice(half * 128, half * 128 + 128)
            cols = slice(part * 256, part * 256 + 256)
            at[dyn(half * 2 + c, 128), cols] = (
                half_ref[part, :, tokens].astype(F32).T.astype(BF16)
            )
            at[dyn(half * 2 + 1 - c, 128), cols] = (
                recv_ref[1 - part, :, tokens].astype(F32).T.astype(BF16)
            )
    finish(loads)
    copies = []
    if len(d1s) > 1:
        copies += run([pltpu.make_async_copy(dec.at[0], dec_out, out_sems.at[3, 0])])
    for n, d1 in enumerate(d1s):
        for d2 in range(4):
            half, j = tile_at(c, x, y, d1, d2)
            rows = dyn(half, 256)
            cols = slice(d2 * 512, d2 * 512 + 512) if len(d1s) == 1 else dyn(j, 512)
            total = dot_nn(at[rows, 0:256], dec[0, :, cols])
            total += dot_nn(at[rows, 256:512], dec[1, :, cols])
            blk[n, d2 // 2, d2 % 2] = total.astype(BF16)
            if d2 % 2 == 1:
                copies += run(
                    [
                        pltpu.make_async_copy(
                            blk.at[n, d2 // 2], outs[2 * n + d2 // 2], out_sems.at[n, d2 // 2]
                        )
                    ]
                )
    finish(copies)


def backward_kernel(parts, d1s, first, *refs):
    e_refs, refs = (refs[0:2], refs[2:4]), refs[4:]
    half_ref, recv_ref, refs = refs[0], refs[1], refs[2:]
    dec_refs, refs = refs[: len(parts)], refs[len(parts) :]
    if not first:
        d_ins, refs = refs[: len(parts)], refs[len(parts) :]
    d_outs, refs = refs[: len(parts)], refs[len(parts) :]
    g_outs, refs = refs[: len(parts)], refs[len(parts) :]
    err, dec, af, g_blk, sems, w_sems, out_sems = refs
    c, x, y = place()
    copies = []
    for i, pair in enumerate(e_refs):
        for d2 in range(4):
            half, jj = tile_in_pair(c, x, d1s, i, d2)
            copies.append(
                pltpu.make_async_copy(
                    pair[d2 // 2].at[d2 % 2],
                    err.at[jj, dyn(half, 256), :],
                    sems.at[i * 4 + d2],
                )
            )
    run(copies)
    loads = []
    for n, part in enumerate(parts):
        for jj in range(4):
            j = pair_block(c, x, y, d1s, jj)
            loads.append(
                pltpu.make_async_copy(
                    dec_refs[n].at[:, dyn(j, 512)],
                    dec.at[n, :, jj * 512 : jj * 512 + 512],
                    w_sems.at[n, jj],
                )
            )
    run(loads)
    for n, part in enumerate(parts):
        for half in range(2):
            tokens = slice(half * 128, half * 128 + 128)
            af[n, :, dyn(half * 2 + c, 128)] = half_ref[part, :, tokens]
            af[n, :, dyn(half * 2 + 1 - c, 128)] = recv_ref[1 - part, :, tokens]
    finish(copies)
    finish(loads)
    outs = []
    for n, part in enumerate(parts):
        total = None if first else d_ins[n][:, 0:512]
        square = 0.0 if first else d_ins[n][:, 512:513]
        for jj in range(4):
            cols = slice(jj * 512, jj * 512 + 512)
            g = dot_nn(af[n], err[jj])
            g_blk[n, :, cols] = g.astype(BF16)
            square = square + jnp.sum(g * g, axis=1, keepdims=True)
            outs += run(
                [
                    pltpu.make_async_copy(
                        g_blk.at[n, :, cols], g_outs[n].at[:, cols], out_sems.at[n, jj]
                    )
                ]
            )
            term = dot_nt(dec[n, :, cols], err[jj])
            total = term if total is None else total + term
        d_outs[n][:, 0:512] = total
        d_outs[n][:, 512:640] = jnp.broadcast_to(square, (square.shape[0], 128))
    finish(outs)


def step_kernel(
    d_mine, d_got, mask_ref, x_own, x_other, go_a, go_b, gg_a, gg_b, esec, dsec,
    enc_step, dec_step, enc_new, dec_new,
    xs, gs, genc, d_blk, e_blk, sems, g_sems, d_sems, e_sems,
):
    c, x, y = place()
    width = genc.shape[1]
    pairs = ((0, 2), (1, 3))
    x_loads, g_loads, blocks = [], [], []
    for n, (core, xp, gp) in enumerate(
        ((c, x_own, (go_a, go_b)), (1 - c, x_other, (gg_a, gg_b)))
    ):
        for p, d1s in enumerate(pairs):
            g_loads.append(pltpu.make_async_copy(gp[p], gs.at[n, p], g_sems.at[n, p]))
            for jj in range(4):
                j = pair_block(core, x, y, d1s, jj)
                blocks.append((n, p, jj, core, j))
                x_loads.append(
                    pltpu.make_async_copy(
                        xp.at[p, jj], xs.at[n, j], sems.at[n, p * 4 + jj]
                    )
                )
    run(x_loads)
    run(g_loads)
    chosen = mask_ref[0].astype(F32)
    touched = row(jnp.max(chosen, axis=1, keepdims=True)) > 0
    square = row(d_mine[:, 512:513] + d_got[:, 512:513])
    old = dsec[...]
    new = DECAY_RATE * old + (1.0 - DECAY_RATE) * (square / (2 * width))
    v_dec = jnp.where(touched, new, old)
    dec_new[...] = v_dec
    rate_dec = column(jnp.where(touched, -1.0 / (jnp.sqrt(v_dec) + EPSILON), 0.0))
    grad = jnp.where(chosen > 0, d_mine[:, 0:512] + d_got[:, 0:512], 0.0).astype(BF16)
    by_core = [
        jnp.concatenate([grad[:, 0:128], grad[:, 256:384]], 1),
        jnp.concatenate([grad[:, 128:256], grad[:, 384:512]], 1),
    ]
    dact = [
        jnp.where(c == 0, by_core[0], by_core[1]),
        jnp.where(c == 0, by_core[1], by_core[0]),
    ]
    finish(x_loads)
    finish(g_loads)
    outs = []
    total = 0.0
    for j in range(8):
        cols = slice(j * 512, j * 512 + 512)
        g = dot_nn(dact[0], xs[0, j]) + dot_nn(dact[1], xs[1, j])
        genc[:, cols] = g
        total = total + jnp.sum(g * g, axis=1, keepdims=True)
        for n, p, jj, core, block in blocks[2 * j : 2 * j + 2]:
            part = slice(jj * 512, jj * 512 + 512)
            d_blk[n, p, :, part] = (gs[n, p, :, part].astype(F32) * rate_dec).astype(BF16)
            outs += run(
                [
                    pltpu.make_async_copy(
                        d_blk.at[n, p, :, part],
                        dec_step.at[:, dyn(slot_of(core) * 8 + block, 512)],
                        d_sems.at[n, p * 4 + jj],
                    )
                ]
            )
    old = esec[...]
    new = DECAY_RATE * old + (1.0 - DECAY_RATE) * (row(total) / width)
    v_enc = jnp.where(touched, new, old)
    enc_new[...] = v_enc
    rate_enc = column(jnp.where(touched, -1.0 / (jnp.sqrt(v_enc) + EPSILON), 0.0))
    for j in range(4):
        cols = slice(j * 1024, j * 1024 + 1024)
        e_blk[:, cols] = (genc[:, cols] * rate_enc).astype(BF16)
        outs += run(
            [pltpu.make_async_copy(e_blk.at[:, cols], enc_step.at[:, cols], e_sems.at[j])]
        )
    finish(outs)


def body(resid, target, feat_idx, enc_weight, enc_bias, dec_weight, enc_second, dec_second):
    l, z = lax.axis_index("l"), lax.axis_index("z")
    xh, xl, c, y = (lax.axis_index(n) for n in ("xh", "xl", "c", "y"))
    is_one = c == 1
    n_f, width = enc_weight.shape

    high = lax.shift_right_logical(feat_idx, 7)
    packed = jnp.concatenate([resid, high.astype(BF16), (feat_idx & 127).astype(BF16)], 1)
    by_z = gather(packed, z_get)
    x_z = jnp.concatenate([p[:, :512] for p in by_z], 0)

    digits = jnp.concatenate([p[:, 512:] for p in by_z], 0)
    digits = digits.astype(jnp.int32)
    idx = digits[:, :64] * 128 + digits[:, 64:]
    other = swap_cores(idx)
    idx = jnp.concatenate([jnp.where(is_one, other, idx), jnp.where(is_one, idx, other)], 0)
    other = lax.ppermute(idx, "xh", [(0, 1), (1, 0)])
    idx = jnp.concatenate([jnp.where(xh == 1, other, idx), jnp.where(xh == 1, idx, other)], 0)
    feat = xl * 4 + y
    member = z * 4 + xh * 2 + c
    mate = z * 4 + xh * 2 + (1 - c)
    bases = jnp.stack([(member * 8 + feat) * n_f, (mate * 8 + feat) * n_f]).astype(jnp.int32)
    mask = call(
        mask_kernel, shape((2, n_f, 512)), [], [SMEM, VMEM], VMEM, 4 * 10**9, 2**20, 4, "mask"
    )(bases, idx.T)

    enc_other = swap_cores(enc_weight)
    bias_other = swap_cores(enc_bias)
    dec_other = swap_cores(lax.dynamic_slice_in_dim(dec_weight, slot_of(1 - c) * width, width, 1))
    x_1 = jnp.stack(gather(x_z, lambda v, d: ring_get(v, 2, d)))
    x_blocks = gather(x_1, lambda v, d: ring_get(v, 1, d))

    def encode(d1s, extra, extra_specs, outs, out_specs, sems):
        first = d1s[0] == 0
        return call(
            lambda *refs: encode_kernel(d1s, first, *refs),
            outs,
            [
                pltpu.VMEM((4, 256, 512), BF16),
                pltpu.VMEM((2, n_f, 2048), BF16),
                DMA((8,)),
                DMA((8,)),
            ]
            + sems,
            [ANY] * 4 + extra_specs,
            out_specs,
            512 * 256 * width,
            4 * 2**20,
            14,
            "encode_near" if first else "encode_far",
        )(x_blocks[d1s[0]], x_blocks[d1s[1]], enc_weight, enc_other, *extra)

    acc = encode(
        (0, 2), (enc_bias[None], bias_other[None]), [VMEM] * 2, shape((2, n_f, 256), F32), VMEM, []
    )
    act_half, x_own = encode(
        (1, 3),
        (acc, mask, x_blocks[0], x_blocks[2]),
        [VMEM, VMEM, ANY, ANY],
        (shape((2, n_f, 256)), shape((2, 4, 256, 512))),
        (VMEM, ANY),
        [DMA((9,))],
    )
    act_recv = swap_cores(act_half)
    x_own, act_recv = lax.optimization_barrier((x_own, act_recv))
    x_other = swap_cores(x_own)

    def decode(d1s):
        wide, extra = (2048, ()) if len(d1s) == 1 else (width, (shape((n_f, width)),))
        return call(
            lambda *refs: decode_kernel(d1s, *refs),
            (shape((2, 256, 512)),) * (2 * len(d1s)) + extra,
            [
                pltpu.VMEM((512, 512), BF16),
                pltpu.VMEM((2, n_f, wide), BF16),
                pltpu.VMEM((len(d1s), 2, 2, 256, 512), BF16),
                DMA((2, 4)),
                DMA((4, 2)),
            ],
            [VMEM, VMEM, ANY, ANY],
            (ANY,) * (2 * len(d1s) + len(extra)),
            2 * 512 * 128 * width * len(d1s),
            4 * 2**20,
            18,
            "decode_far" if len(d1s) == 1 else "decode_near",
        )(act_half, act_recv, dec_weight, dec_other)

    far = decode((2,))
    up_a = ring_put(far[0], 1, 1)
    down_b = ring_put(far[1], 1, 3)
    plus_a, plus_b, minus_a, minus_b, own_a, own_b, dec_own = decode((1, 3, 0))
    own_a, x_other = lax.optimization_barrier((own_a, x_other))
    up_b = ring_put(plus_b, 1, 1)
    down_a = ring_put(minus_a, 1, 3)
    next_a = ring_put((plus_a.astype(F32) + up_a.astype(F32)).astype(BF16), 1, 1)
    next_b = ring_put((minus_b.astype(F32) + down_b.astype(F32)).astype(BF16), 1, 3)

    def scatter(parts, put):
        far = put(parts[2].astype(BF16), 2)
        got = [parts[0], put(parts[1].astype(BF16), 1), far, put(parts[3].astype(BF16), 3)]
        return got

    halves = ((own_a, next_a, down_a), (own_b, next_b, up_b))
    parts = [sum(g[d % 2].astype(F32) for g in halves[d // 2]) for d in range(4)]
    got = scatter(parts, lambda v, d: ring_put(v, 2, d))
    sums = sum(g.astype(F32) for g in got).reshape(2, 4, 32, 512)
    got = scatter([sums[:, d] for d in range(4)], lambda v, d: z_get(v, -d))
    total = sum(g.astype(F32) for g in got)

    other = swap_cores(target)
    tgt = jnp.stack([jnp.where(is_one, other, target), jnp.where(is_one, target, other)])
    tgt_next = lax.ppermute(tgt, ("l", "c"), [(3, 1)])
    tgt = jnp.where(is_one & (l == 0), tgt_next, tgt)
    peer = lax.ppermute(total.astype(BF16), ("l", "c"), [(1, 3), (3, 1)])
    err = (total + peer.astype(F32) - tgt.astype(F32)).astype(BF16)
    err = jnp.where((l == 1) & (c == 0), jnp.zeros_like(err), err)

    err = jnp.stack(gather(err, z_get), 1).reshape(256, 512)
    err = gather(err, lambda v, d: ring_get(v, 2, d))
    err_a, err_b = jnp.stack(err[:2]), jnp.stack(err[2:])
    plus_a = ring_get(err_a, 1, 1)
    minus_b = ring_get(err_b, 1, 3)
    plus_b = ring_get(err_b, 1, 1)
    minus_a = ring_get(err_a, 1, 3)
    far_a = ring_get(plus_a, 1, 1)
    far_b = ring_get(minus_b, 1, 3)

    def backward(parts, d1s, errs, init):
        first = not init
        weights = [(dec_own, dec_other)[p] for p in parts]
        n = len(parts)
        outs = call(
            lambda *refs: backward_kernel(parts, d1s, first, *refs),
            (shape((n_f, 640), F32),) * n + (shape((n_f, 2048)),) * n,
            [
                pltpu.VMEM((4, 512, 512), BF16),
                pltpu.VMEM((n, n_f, 2048), BF16),
                pltpu.VMEM((n, n_f, 512), BF16),
                pltpu.VMEM((n, n_f, 2048), BF16),
                DMA((8,)),
                DMA((n, 4)),
                DMA((n, 4)),
            ],
            [ANY] * 4 + [VMEM] * 2 + [ANY] * n + [VMEM] * len(init),
            (VMEM,) * n + (ANY,) * n,
            2 * n * 512 * 256 * width,
            (2 + 2 * n) * 2**20,
            20,
            "backward_" + "_".join(str(p) for p in parts),
        )(*errs, act_half, act_recv, *weights, *init)
        return outs

    d_own, d_other, go_b, gt_b = backward((0, 1), (1, 3), (plus_a, plus_b, minus_a, minus_b), ())
    gg_b = swap_cores(gt_b)
    near = (err_a, err_b, far_a, far_b)
    d_other, gt_a = backward((1,), (0, 2), near, (d_other,))
    d_got = swap_cores(d_other)
    gg_a = swap_cores(gt_a)
    d_own, go_a = backward((0,), (0, 2), near, (d_own,))
    enc_step, dec_step, enc_new, dec_new = call(
        step_kernel,
        (
            shape((n_f, width)), shape((n_f, 2 * width)),
            shape((1, n_f), F32), shape((1, n_f), F32),
        ),
        [
            pltpu.VMEM((2, 8, 256, 512), BF16),
            pltpu.VMEM((2, 2, n_f, 2048), BF16),
            pltpu.VMEM((n_f, width), F32),
            pltpu.VMEM((2, 2, n_f, 2048), BF16),
            pltpu.VMEM((n_f, width), BF16),
            DMA((2, 8)),
            DMA((2, 2)),
            DMA((2, 8)),
            DMA((4,)),
        ],
        [VMEM] * 3 + [ANY] * 6 + [VMEM] * 2,
        (ANY, ANY, VMEM, VMEM),
        2 * 512 * 256 * width,
        14 * 2**20,
        34,
        "steps",
    )(
        d_own, d_got, mask, x_own, x_other, go_a, go_b, gg_a, gg_b,
        enc_second[None], dec_second[None],
    )
    return enc_step, dec_step, enc_new.reshape(n_f), dec_new.reshape(n_f)


def solution(mesh):
    devices = mesh.devices.reshape(2, 4, 2, 2, 2, 4)
    fine = Mesh(devices, ("l", "z", "xh", "c", "xl", "y"))
    rows, cols = ("l", "z", "xh", "c"), ("xl", "y")
    in_specs = (
        P(rows, cols),
        P(rows, cols),
        P(rows, None),
        P(rows + cols, None),
        P(rows + cols),
        P(rows + cols, None),
        P(rows + cols),
        P(rows + cols),
    )
    out_specs = (P(rows + cols, None), P(rows + cols, None), P(rows + cols), P(rows + cols))
    return jax.shard_map(body, mesh=fine, in_specs=in_specs, out_specs=out_specs, check_vma=False)
```
